1024 devices in a mesh: dp: 64 (over x, z_lo), fsdp: 16 (over z_hi, y, core).
Axes of the slice: x: 4, y: 4, z: 32 (z_hi: 2, z_lo: 16; z = z_hi * 16 + z_lo), core: 2. Of those that a mesh axis runs over, the one named last changes fastest.
Arguments:
- embeddings: bfloat16 [1024, 256, 256], P(('dp', 'fsdp')), may hold values from -6 to 6
- cotangent: bfloat16 [1024, 256, 256], P(('dp', 'fsdp')), may hold values from -24 to 24
- owners: int32 [1024, 256], P(('dp', 'fsdp')), may hold values from 0 to 63, as said below
- projection: bfloat16 [256, 128], P('fsdp'), may hold values from -0.375 to 0.375
- up_weight: bfloat16 [128, 4096], P('fsdp'), may hold values from -0.5 to 0.5
- down_weight: bfloat16 [4096, 256], P('fsdp'), may hold values from -0.09375 to 0.09375
Outputs:
- owned_grads: bfloat16 [262144, 256], P(('dp', 'fsdp'))
- grad_projection: float32 [256, 128], P('fsdp')
- grad_up: float32 [128, 4096], P('fsdp')
- grad_down: float32 [4096, 256], P('fsdp')
The draws below stay inside these ranges and needn't reach their ends.
Inputs may be any that keep to these rules, and one draw needn't show every extreme that they name: `owners`: among the rows (samples by features) of one device, every owner appears exactly 1 * 256 / 64 times.
All inputs are finite; a program needn't handle non-finite values.
Results may differ from the reference program's by a relative error of at most 0.018.
Values may be sent and summed in bfloat16 or wider, within the bound.
A program may use at most 32 MiB of HBM per device.

```python
import jax
import jax.numpy as jnp
from jax import lax

F = 256
D = 256
K = 128
H = 4096
SAMP_DEV = 1
SAMPLES = 1024
N_DP = 64
N_FSDP = 16


def draw_owners(key, part):
    key = jax.random.fold_in(key, 7)
    rows = SAMP_DEV * F
    blocks = SAMPLES // SAMP_DEV
    keys = jax.random.split(key, blocks)
    perms = jax.vmap(lambda k: jax.random.permutation(k, rows))(keys)
    return (perms % N_DP).reshape(SAMPLES, F).astype(jnp.int32)


def with_spikes(drawn, own_key, source, target, shards_of, factor):
    def block_of(axis_at):
        return (jnp.arange(drawn.shape[axis_at]) // (drawn.shape[axis_at] // shards_of)).reshape((-1,) + (1,) * (drawn.ndim - 1 - axis_at))

    first = jax.random.permutation(own_key, shards_of)[block_of(target)]
    far = (block_of(target) + shards_of // 2) % shards_of
    return jnp.where((block_of(source) == first) | (block_of(source) == far), factor * drawn, drawn)


def block_scale(key, dims, shards, low, high):
    loudness = 1.0
    for position, parts in shards:
        heights = jax.random.uniform(jax.random.fold_in(jax.random.fold_in(key, 6), position), (parts,), jnp.float32, low / len(shards), high / len(shards))
        loudness = loudness * jnp.repeat(jnp.exp(heights), dims[position] // parts).reshape((-1,) + (1,) * (len(dims) - 1 - position))
    return loudness


def scatter_about(rng, dims, scale, most, cuts=(), held_as=jnp.bfloat16):
    level = block_scale(rng, dims, cuts, -0.22, 0.18) if cuts else 1.0
    values = jax.random.normal(rng, dims, jnp.float32) * scale * level
    return jnp.minimum(jnp.maximum(values, -most), most).astype(held_as)


def bell_draw_with(rng, shape, scale, most, shards, heavy, dtype=jnp.bfloat16):
    values = scale * jax.random.normal(rng, shape, jnp.float32)
    if shards:
        values = values * block_scale(rng, shape, shards, -0.22, 0.18)
    return jnp.clip(with_spikes(values, jax.random.fold_in(rng, 3), *heavy), -most, most).astype(dtype)


def setup_inputs(seed: int = 0) -> dict:
    key_list = jax.random.split(jax.random.key(seed), 7)
    return {
        "embeddings": scatter_about(key_list[0], (SAMPLES, F, D), 1.0, 6.0, ((0, 1024),)),
        "cotangent": bell_draw_with(key_list[1], (SAMPLES, F, D), 1.0, 24.0, ((0, 1024),), (0, 1, 256, 6.0)),
        "owners": draw_owners(jax.random.fold_in(key_list[6], 71), 0),
        "projection": scatter_about(key_list[3], (F, K), F ** -0.5, 0.375, ((0, 16),)),
        "up_weight": scatter_about(key_list[4], (K, H), K ** -0.5, 0.5, ((0, 16),)),
        "down_weight": scatter_about(key_list[5], (H, D), H ** -0.5, 0.09375, ((0, 16),)),
    }


def local_backward(emb, cot, proj, w_up, w_down):
    samples, feats, width = emb.shape
    rank = proj.shape[1]
    compressed = jnp.einsum('sfd,fk->sdk', emb.astype(jnp.float32), proj.astype(jnp.float32)).astype(jnp.bfloat16)
    fm_vals = jnp.einsum('sfd,sdk->sfk', emb.astype(jnp.float32), compressed.astype(jnp.float32))
    centre = fm_vals - lax.optimization_barrier(jnp.mean(fm_vals, axis=-1, keepdims=True))
    inv = lax.rsqrt(lax.optimization_barrier(jnp.mean(centre * centre, axis=-1, keepdims=True)) + 1e-05)
    normed = centre * inv
    normed_low = normed.astype(jnp.bfloat16).reshape(samples * feats, rank)
    cot_rows = cot.reshape(samples * feats, width)
    hidden = jnp.dot(normed_low, w_up, preferred_element_type=jnp.float32)
    sig = jax.nn.sigmoid(hidden)
    activated = (hidden * sig).astype(jnp.bfloat16)
    grad_act = jnp.dot(cot_rows, w_down.T, preferred_element_type=jnp.float32)
    grad_hidden = (grad_act * sig * (1.0 + hidden * (1.0 - sig))).astype(jnp.bfloat16)
    grad_normed = jnp.dot(grad_hidden, w_up.T, preferred_element_type=jnp.float32).reshape(samples, feats, rank)
    grad_fm = inv * (grad_normed - lax.optimization_barrier(jnp.mean(grad_normed, axis=-1, keepdims=True)) - normed * lax.optimization_barrier(jnp.mean(grad_normed * normed, axis=-1, keepdims=True)))
    grad_fm = grad_fm.astype(jnp.bfloat16)
    grad_comp = jnp.einsum('sfd,sfk->sdk', emb.astype(jnp.float32), grad_fm.astype(jnp.float32)).astype(jnp.bfloat16)
    grad_embed = (jnp.einsum('sfk,sdk->sfd', grad_fm.astype(jnp.float32), compressed.astype(jnp.float32)) + jnp.einsum('fk,sdk->sfd', proj.astype(jnp.float32), grad_comp.astype(jnp.float32))).astype(jnp.bfloat16)
    part_up = jnp.dot(normed_low.T, grad_hidden, preferred_element_type=jnp.float32)
    part_down = jnp.dot(activated.T, cot_rows, preferred_element_type=jnp.float32)
    part_proj = jnp.einsum('sfd,sdk->fk', emb.astype(jnp.float32), grad_comp.astype(jnp.float32))
    return (grad_embed, part_proj, part_up, part_down)

def reference(embeddings, cotangent, owners, projection, up_weight, down_weight):
    devices = N_DP * N_FSDP
    emb_dev = embeddings.reshape(devices, SAMP_DEV, F, D)
    cot_dev = cotangent.reshape(devices, SAMP_DEV, F, D)

    def step(carry, pieces):
        grad_embed, part_proj, part_up, part_down = local_backward(pieces[0], pieces[1], projection, up_weight, down_weight)
        carry = (carry[0] + part_proj.astype(jnp.bfloat16).astype(jnp.float32), carry[1] + part_up.astype(jnp.bfloat16).astype(jnp.float32), carry[2] + part_down.astype(jnp.bfloat16).astype(jnp.float32))
        return (carry, grad_embed)
    start = (jnp.zeros((F, K), jnp.float32), jnp.zeros((K, H), jnp.float32), jnp.zeros((H, D), jnp.float32))
    totals, grad_embed = lax.scan(step, start, (emb_dev, cot_dev))
    rows = SAMP_DEV * F
    per_owner = rows // N_DP
    grad_rows = grad_embed.reshape(N_DP, N_FSDP, rows, D)
    owner_rows = owners.reshape(N_DP, N_FSDP, rows).astype(jnp.int32)
    order = jnp.argsort(owner_rows, axis=-1, stable=True).astype(jnp.int32)
    ordered = jnp.take_along_axis(grad_rows, order[..., None], axis=2)
    ordered = ordered.reshape(N_DP, N_FSDP, N_DP, per_owner, D)
    owned = jnp.transpose(ordered, (2, 1, 0, 3, 4)).reshape(SAMPLES * F, D)
    scale = 1.0 / SAMPLES
    return (owned, totals[0] * scale, totals[1] * scale, totals[2] * scale)
```

```python
import functools

import jax
import jax.numpy as jnp
from jax import lax
from jax.experimental import pallas as pl
from jax.experimental.pallas import tpu as pltpu
from jax.sharding import PartitionSpec as P

BF = jnp.bfloat16
F32 = jnp.float32
SPLITS = {64: (4, 16, 4), 4: (2, 2, 2), 8: (2, 4, 2)}
NZH, NY, NC = 2, 4, 2
NF = NZH * NY * NC
MAIN, ROWS = 768, 784


def mm(a, b, ca=1, cb=0):
    return lax.dot_general(a, b, (((ca,), (cb,)), ((), ())), preferred_element_type=F32)


def kernel(
    split, x_ref, cot_ref, own_ref, proj_ref, up_ref, dn_ref,
    owned_ref, gproj_ref, gup_ref, gdn_ref,
    wg, gg, rc, sa, ry, sb, rx, sc, rq, se, rb, ox, nl, gn, av1, av2, av3, av4,
    ag_s, ag_r, rs_s, rs_r, aa_s, aa_r,
):
    nx, nzl, nq = split
    nb = nzl // nq
    feats = x_ref.shape[1]
    xp = rx.shape[2]
    bp = rb.shape[1]
    qp = nb * bp
    zrows = feats // nzl
    per = zrows // nx
    dp, fs = lax.axis_index("dp"), lax.axis_index("fsdp")
    x, zl = dp // nzl, dp % nzl
    zh, y, c = fs // (NY * NC), (fs // NC) % NY, fs % NC
    q, b = zl % nq, zl // nq

    def dev(x=x, zl=zl, zh=zh, y=y, c=c):
        return {"dp": x * nzl + zl, "fsdp": (zh * NY + y) * NC + c}

    pending = []

    def send(src, dst, sems, to):
        ssem, rsem, i = sems
        copy = pltpu.make_async_remote_copy(
            src_ref=src, dst_ref=dst, send_sem=ssem.at[i], recv_sem=rsem.at[i],
            device_id=to, device_id_type=pl.DeviceIdType.MESH,
        )
        copy.start()
        pending.append(copy)
        return copy

    barrier = pltpu.get_barrier_semaphore()
    peers = [dev(c=1 - c)]
    peers += [dev(y=(y + k) % NY) for k in range(1, NY)]
    peers += [dev(x=(x + k) % nx) for k in range(1, nx)]
    peers += [dev(zl=(zl + k) % nzl) for k in range(1, nzl)]
    peers += [dev(zh=1 - zh, zl=((b + k) % nb) * nq + q) for k in range(nb)]
    peers += [dev(zh=1 - zh, zl=nzl - 1 - zl)]
    for p in peers:
        pl.semaphore_signal(barrier, inc=1, device_id=p, device_id_type=pl.DeviceIdType.MESH)

    wg[fs, 0:256] = dn_ref[:, 0:128]
    wg[fs, 256:512] = dn_ref[:, 128:256]
    for u in range(NF):
        lo = up_ref[:, 256 * u : 256 * u + 128].astype(F32)
        hi = up_ref[:, 256 * u + 128 : 256 * u + 256].astype(F32)
        wg[fs, 512 + 16 * u : 528 + 16 * u] = jnp.concatenate([lo, hi], axis=0).astype(BF)
    wg[fs, MAIN:ROWS] = proj_ref[...]
    pl.semaphore_wait(barrier, len(peers))

    part = MAIN // (nx * nq)
    fp = fs + (1 - 2 * zh) * NY * NC
    mq = nq - 1 - q
    piece = pl.ds(pl.multiple_of((x * nq + mq) * part, 16), part)
    n_ag = 0
    across = [
        send(wg.at[fs, piece], wg.at[fs, piece], (ag_s, ag_r, 0), dev(zh=1 - zh, zl=nzl - 1 - zl)),
        send(wg.at[fs, MAIN:ROWS], wg.at[fs, MAIN:ROWS], (ag_s, ag_r, 1), dev(zh=1 - zh, zl=nzl - 1 - zl)),
    ]
    n_ag = 2
    ycopies = []
    for k in (1, 3, 2):
        ycopies.append((k, fs, send(wg.at[fs], wg.at[fs], (ag_s, ag_r, n_ag), dev(y=(y + k) % NY))))
        n_ag += 1
    ccopies = [send(wg.at[fs], wg.at[fs], (ag_s, ag_r, n_ag), dev(c=1 - c))]
    n_ag += 1
    across[0].wait_recv()
    piece = pl.ds(pl.multiple_of((x * nq + q) * part, 16), part)
    step = []
    for k in range(1, nq):
        step.append(send(wg.at[fp, piece], wg.at[fp, piece], (ag_s, ag_r, n_ag), dev(zl=b * nq + (q + k) % nq)))
        n_ag += 1
    for s in step:
        s.wait_recv()
    piece = pl.ds(pl.multiple_of(x * nq * part, 16), nq * part)
    step = []
    for k in range(1, nx):
        step.append(send(wg.at[fp, piece], wg.at[fp, piece], (ag_s, ag_r, n_ag), dev(x=(x + k) % nx)))
        n_ag += 1
    for s in step:
        s.wait_recv()
    across[1].wait_recv()
    for k in (1, 3, 2):
        ycopies.append((k, fp, send(wg.at[fp], wg.at[fp], (ag_s, ag_r, n_ag), dev(y=(y + k) % NY))))
        n_ag += 1
    ccopies.append(send(wg.at[fp], wg.at[fp], (ag_s, ag_r, n_ag), dev(c=1 - c)))
    n_ag += 1
    for k, base, copy in ycopies:
        copy.wait_recv()
        got = base + (((y - k + NY) % NY) - y) * NC
        ccopies.append(send(wg.at[got], wg.at[got], (ag_s, ag_r, n_ag), dev(c=1 - c)))
        n_ag += 1
    for s in ccopies:
        s.wait_recv()

    emb, cot = x_ref[0], cot_ref[0]
    proj = wg[:, MAIN:ROWS, :].reshape(feats, 128)
    compressed = mm(emb, proj, 0, 0).astype(BF)
    fm = mm(emb, compressed)
    centre = fm - jnp.mean(fm, axis=-1, keepdims=True)
    inv = lax.rsqrt(jnp.mean(centre * centre, axis=-1, keepdims=True) + 1e-05)
    normed = centre * inv
    nl[...] = normed.astype(BF)
    gn[...] = jnp.zeros_like(gn)

    @pl.loop(0, NF)
    def _(u):
        urows = pl.ds(pl.multiple_of(512 + 16 * u, 16), 16)
        pieces = wg[:, urows, :].astype(F32)
        up = jnp.concatenate(
            [pieces[:, 0:8].reshape(128, 128), pieces[:, 8:16].reshape(128, 128)], axis=1
        ).astype(BF)
        down = jnp.concatenate([wg[u, 0:256], wg[u, 256:512]], axis=1)
        low, cots = nl[...], cot_ref[0]
        hidden = mm(low, up)
        sig = 0.5 * jnp.tanh(0.5 * hidden) + 0.5
        act = (hidden * sig).astype(BF)
        gh = (mm(cots, down, 1, 1) * sig * (1.0 + hidden * (1.0 - sig))).astype(BF)
        gn[...] += mm(gh, up, 1, 1)
        gup = mm(low, gh, 0, 0)
        gup = jnp.concatenate(
            [gup[:, 0:128].reshape(NF, 8, 128), gup[:, 128:256].reshape(NF, 8, 128)], axis=1
        ).astype(BF)
        gg[:, :, :, urows, :] = gup.reshape(NZH, NY, NC, 16, 128)
        gdn = mm(act, cots, 0, 0).astype(BF)
        at = (u // (NY * NC), (u // NC) % NY, u % NC)
        gg[at[0], at[1], at[2], 0:256] = gdn[:, 0:128]
        gg[at[0], at[1], at[2], 256:512] = gdn[:, 128:256]

    rs = 0
    main = pl.ds(0, MAIN)
    tail = pl.ds(MAIN, ROWS - MAIN)
    r0 = [send(gg.at[:, :, 1 - c, main], rc.at[:, :, main], (rs_s, rs_r, rs), dev(c=1 - c))]
    rs += 1

    gnorm = gn[...]
    gfm = inv * (
        gnorm
        - jnp.mean(gnorm, axis=-1, keepdims=True)
        - normed * jnp.mean(gnorm * normed, axis=-1, keepdims=True)
    )
    gfm = gfm.astype(BF)
    gcomp = mm(emb, gfm, 0, 0).astype(BF)
    gproj = mm(emb, gcomp).astype(BF)
    gg[:, :, :, MAIN:ROWS, :] = gproj.reshape(NZH, NY, NC, 16, 128)
    r0.append(send(gg.at[:, :, 1 - c, tail], rc.at[:, :, tail], (rs_s, rs_r, rs), dev(c=1 - c)))
    rs += 1
    gemb = (mm(gfm, compressed, 1, 1) + mm(proj, gcomp, 1, 1)).astype(BF)

    row = lax.broadcasted_iota(jnp.int32, (feats, feats), 0)
    col = lax.broadcasted_iota(jnp.int32, (feats, feats), 1)
    across_f = jnp.broadcast_to(own_ref[...].astype(F32), (feats, feats))
    down_f = jnp.sum(jnp.where(row == col, across_f, 0.0), axis=1, keepdims=True)
    within = jnp.sum(
        jnp.where((across_f == down_f) & (row < col), 1.0, 0.0), axis=0, keepdims=True
    )
    owner = across_f[0:1]
    owner_x = jnp.floor(owner * (1.0 / nzl))
    place = (owner - owner_x * nzl) * zrows + owner_x * per + within
    perm = jnp.where(row.astype(F32) == place, 1.0, 0.0).astype(BF)
    av1[...] = mm(perm, gemb).astype(BF)
    a1 = []
    mine = pl.ds(pl.multiple_of(zl * zrows, 16), zrows)
    aa = 0
    for k in range(1, nzl):
        to = (zl + k) % nzl
        theirs = pl.ds(pl.multiple_of(to * zrows, 16), zrows)
        a1.append(send(av1.at[theirs], av2.at[mine], (aa_s, aa_r, aa), dev(zl=to)))
        aa += 1
    av2[mine] = av1[mine]

    for s in r0:
        s.wait_recv()
    blk = 112
    r1 = []
    for k in (1, 3, 2, 0):
        to = (y + k) % NY

        @pl.loop(0, ROWS // blk)
        def _(i, to=to):
            r = pl.ds(pl.multiple_of(i * blk, 16), blk)
            sa[to, :, r] = (gg[:, to, c, r].astype(F32) + rc[:, to, r].astype(F32)).astype(BF)

        if k:
            r1.append(send(sa.at[to], ry.at[k - 1], (rs_s, rs_r, rs), dev(y=to)))
            rs += 1

    for s in a1:
        s.wait_recv()
    r_z, r_x, r_k = col // zrows, (col % zrows) // per, col % per
    perm = jnp.where(row == r_x * (nzl * per) + r_z * per + r_k, 1.0, 0.0).astype(BF)
    av3[...] = mm(perm, av2[...]).astype(BF)
    a2 = []
    xrows = nzl * per
    mine = pl.ds(pl.multiple_of(x * xrows, 16), xrows)
    for k in range(1, nx):
        to = (x + k) % nx
        theirs = pl.ds(pl.multiple_of(to * xrows, 16), xrows)
        a2.append(send(av3.at[theirs], av4.at[mine], (aa_s, aa_r, aa), dev(x=to)))
        aa += 1
    av4[mine] = av3[mine]

    for s in r1:
        s.wait_recv()
    if sb.shape[1] > ROWS:
        sb[:, ROWS:] = jnp.zeros((NZH, sb.shape[1] - ROWS, 128), BF)

    @pl.loop(0, ROWS // blk)
    def _(i):
        r = pl.ds(pl.multiple_of(i * blk, 16), blk)
        t = sa[y, :, r].astype(F32)
        for k in range(NY - 1):
            t += ry[k, :, r].astype(F32)
        sb[:, r] = t.astype(BF)

    r2 = []
    for k in range(1, nx):
        to = (x + k) % nx
        theirs = pl.ds(pl.multiple_of(to * xp, 16), xp)
        r2.append(send(sb.at[:, theirs], rx.at[k - 1], (rs_s, rs_r, rs), dev(x=to)))
        rs += 1
    for s in r2:
        s.wait_recv()
    t = sb[:, pl.ds(pl.multiple_of(x * xp, 16), xp)].astype(F32)
    for k in range(nx - 1):
        t += rx[k].astype(F32)
    sc[:, 0:xp] = t.astype(BF)
    if sc.shape[1] > xp:
        sc[:, xp:] = jnp.zeros((NZH, sc.shape[1] - xp, 128), BF)

    r3 = []
    for k in range(1, nq):
        to = (q + k) % nq
        theirs = pl.ds(pl.multiple_of(to * qp, 16), qp)
        r3.append(send(sc.at[:, theirs], rq.at[k - 1], (rs_s, rs_r, rs), dev(zl=b * nq + to)))
        rs += 1
    for s in r3:
        s.wait_recv()
    t = sc[:, pl.ds(pl.multiple_of(q * qp, 16), qp)].astype(F32)
    for k in range(nq - 1):
        t += rq[k].astype(F32)
    se[...] = t.astype(BF)

    r4 = []
    for k in range(1, NZH * nb):
        h2, b2 = (zh + k // nb) % NZH, (b + k % nb) % nb
        theirs = pl.ds(pl.multiple_of(b2 * bp, 16), bp)
        r4.append(send(se.at[h2, theirs], rb.at[k - 1], (rs_s, rs_r, rs), dev(zh=h2, zl=b2 * nq + q)))
        rs += 1
    for s in r4:
        s.wait_recv()
    mine = pl.ds(pl.multiple_of(b * bp, 16), bp)
    t = se[zh, mine].astype(F32)
    for k in range(NZH * nb - 1):
        t += rb[k].astype(F32)
    ox[x, q, mine] = t.astype(BF)

    for ref, peer_ids in (
        (ox.at[x, q, mine], [dev(zl=((b + k) % nb) * nq + q) for k in range(1, nb)]),
        (ox.at[x, q], [dev(zl=b * nq + (q + k) % nq) for k in range(1, nq)]),
        (ox.at[x], [dev(x=(x + k) % nx) for k in range(1, nx)]),
    ):
        step = []
        for p in peer_ids:
            step.append(send(ref, ref, (rs_s, rs_r, rs), p))
            rs += 1
        for s in step:
            s.wait_recv()

    for s in a2:
        s.wait_recv()
    owned_ref[...] = av4[...]
    scale = 1.0 / (nx * nzl * NF)

    def unit(i):
        at = i * 16
        px, at = at // xp, at % xp
        return ox[px, at // qp, at % qp : at % qp + 16, :].astype(F32) * scale

    for i in range(16):
        gdn_ref[16 * i : 16 * i + 16, 0:128] = unit(i)
        gdn_ref[16 * i : 16 * i + 16, 128:256] = unit(16 + i)
        t = unit(32 + i)
        gup_ref[:, 256 * i : 256 * i + 128] = t[0:8]
        gup_ref[:, 256 * i + 128 : 256 * i + 256] = t[8:16]
    gproj_ref[...] = unit(48)
    for s in pending:
        s.wait_send()


def per_device(split, embeddings, cotangent, owners, projection, up_weight, down_weight):
    nx, nzl, nq = split
    nb = nzl // nq
    feats, width = embeddings.shape[1:]
    units = ROWS // 16
    xu = -(-units // nx)
    bu = -(-xu // (nq * nb))
    xp, bp = 16 * xu, 16 * bu
    qp = nb * bp
    n_ag = 6 + (nq - 1) + (nx - 1) + 4 + 6
    n_rs = 2 + 3 + (nx - 1) * 2 + (nq - 1) * 2 + (NZH * nb - 1) + (nb - 1)
    n_aa = nzl - 1 + nx - 1
    vmem = pl.BlockSpec(memory_space=pltpu.VMEM)
    return pl.pallas_call(
        functools.partial(kernel, split),
        out_shape=(
            jax.ShapeDtypeStruct((feats, width), BF),
            jax.ShapeDtypeStruct(projection.shape, F32),
            jax.ShapeDtypeStruct(up_weight.shape, F32),
            jax.ShapeDtypeStruct(down_weight.shape, F32),
        ),
        in_specs=[vmem] * 6,
        out_specs=(vmem,) * 4,
        scratch_shapes=[
            pltpu.VMEM((NF, ROWS, 128), BF),
            pltpu.VMEM((NZH, NY, NC, ROWS, 128), BF),
            pltpu.VMEM((NZH, NY, ROWS, 128), BF),
            pltpu.VMEM((NY, NZH, ROWS, 128), BF),
            pltpu.VMEM((NY - 1, NZH, ROWS, 128), BF),
            pltpu.VMEM((NZH, nx * xp, 128), BF),
            pltpu.VMEM((nx - 1, NZH, xp, 128), BF),
            pltpu.VMEM((NZH, nq * qp, 128), BF),
            pltpu.VMEM((nq - 1, NZH, qp, 128), BF),
            pltpu.VMEM((NZH, qp, 128), BF),
            pltpu.VMEM((NZH * nb - 1, bp, 128), BF),
            pltpu.VMEM((nx, nq, qp, 128), BF),
            pltpu.VMEM((feats, 128), BF),
            pltpu.VMEM((feats, 128), F32),
            pltpu.VMEM((feats, width), BF),
            pltpu.VMEM((feats, width), BF),
            pltpu.VMEM((feats, width), BF),
            pltpu.VMEM((feats, width), BF),
            pltpu.SemaphoreType.DMA((n_ag,)),
            pltpu.SemaphoreType.DMA((n_ag,)),
            pltpu.SemaphoreType.DMA((n_rs,)),
            pltpu.SemaphoreType.DMA((n_rs,)),
            pltpu.SemaphoreType.DMA((n_aa,)),
            pltpu.SemaphoreType.DMA((n_aa,)),
        ],
        compiler_params=pltpu.CompilerParams(
            collective_id=0, has_side_effects=True, vmem_limit_bytes=48 * 1024 * 1024
        ),
        name="layer_backward",
    )(embeddings, cotangent, owners, projection, up_weight, down_weight)


def solution(mesh):
    return jax.shard_map(
        functools.partial(per_device, SPLITS[mesh.shape["dp"]]),
        mesh=mesh,
        in_specs=(
            P(("dp", "fsdp"), None, None),
            P(("dp", "fsdp"), None, None),
            P(("dp", "fsdp"), None),
            P("fsdp", None),
            P("fsdp", None),
            P("fsdp", None),
        ),
        out_specs=(P(("dp", "fsdp"), None), P("fsdp", None), P("fsdp", None), P("fsdp", None)),
        check_vma=False,
    )
```

```python
import functools

import jax
import jax.numpy as jnp
from jax import lax
from jax.experimental import pallas as pl
from jax.experimental.pallas import tpu as pltpu
from jax.sharding import PartitionSpec as P

BF = jnp.bfloat16
F32 = jnp.float32
SPLITS = {64: (4, 16, 4), 4: (2, 2, 2), 8: (2, 4, 2)}
NZH, NY, NC = 2, 4, 2
NF = NZH * NY * NC
MAIN, ROWS, CUT = 768, 784, 384


def mm(a, b, ca=1, cb=0):
    return lax.dot_general(a, b, (((ca,), (cb,)), ((), ())), preferred_element_type=F32)


def kernel(
    split, x_hbm, cot_hbm, own_hbm, proj_hbm, up_hbm, dn_hbm,
    owned_ref, gproj_ref, gup_ref, gdn_ref,
    x_ref, cot_ref, own_ref, up_ref,
    wg, gg, rc, sa, rya, sba, rxa, rxb, sbb, ryb, sc, rq, se, rb, ox,
    nl, nlt, gn, av1, av2, av3, av4,
    in_s, ag_s, ag_r, co_s, co_r, rs_s, rs_r, aa_s, aa_r,
):
    nx, nzl, nq = split
    nb = nzl // nq
    feats = x_ref.shape[0]
    xa, xb = rxa.shape[2], rxb.shape[3]
    xp, qp = xa + xb, se.shape[1]
    zrows = feats // nzl
    per = zrows // nx
    dp, fs = lax.axis_index("dp"), lax.axis_index("fsdp")
    x, zl = dp // nzl, dp % nzl
    zh, y, c = fs // (NY * NC), (fs // NC) % NY, fs % NC
    q, b = zl % nq, zl // nq

    def dev(x=x, zl=zl, zh=zh, y=y, c=c):
        return {"dp": x * nzl + zl, "fsdp": (zh * NY + y) * NC + c}

    pending = []

    def remote(src, dst, ssem, rsem, i, to):
        return pltpu.make_async_remote_copy(
            src_ref=src, dst_ref=dst, send_sem=ssem.at[i], recv_sem=rsem.at[i],
            device_id=to, device_id_type=pl.DeviceIdType.MESH,
        )

    def sender(ssem, rsem):
        count = [0]

        def send(src, dst, to):
            copy = remote(src, dst, ssem, rsem, count[0], to)
            count[0] += 1
            copy.start()
            pending.append(copy)
            return copy

        return send

    def rows(start, size):
        return pl.ds(pl.multiple_of(start, 16), size)

    gather, reduce, exchange = sender(ag_s, ag_r), sender(rs_s, rs_r), sender(aa_s, aa_r)
    sibling = dev(c=1 - c)
    near_y = {k: dev(y=(y + k) % NY) for k in (1, 3, 2)}
    near_x = {k: dev(x=(x + k) % nx) for k in range(1, nx)}

    barrier = pltpu.get_barrier_semaphore()
    peers = [sibling]
    peers += [
        dev(x=(x + i) % nx, y=(y + k) % NY) for i in range(nx) for k in range(NY) if i or k
    ]
    peers += [dev(zl=(zl + k) % nzl) for k in range(1, nzl)]
    peers += [dev(zh=1 - zh, zl=((b + k) % nb) * nq + q) for k in range(nb)]
    half = ((zl + nzl // 2) % nzl)
    if (nzl // 2) % nq:
        peers.append(dev(zh=1 - zh, zl=half))
    for p in peers:
        pl.semaphore_signal(barrier, inc=1, device_id=p, device_id_type=pl.DeviceIdType.MESH)

    inputs = [
        pltpu.make_async_copy(src, dst, in_s.at[i])
        for i, (src, dst) in enumerate(
            (
                (up_hbm, up_ref),
                (proj_hbm, wg.at[zh, y, c, MAIN:ROWS]),
                (dn_hbm.at[:, 0:128], wg.at[zh, y, c, 0:256]),
                (dn_hbm.at[:, 128:256], wg.at[zh, y, c, 256:512]),
                (x_hbm.at[0], x_ref),
                (own_hbm, own_ref),
                (cot_hbm.at[0], cot_ref),
            )
        )
    ]
    for copy in inputs:
        copy.start()
    inputs[0].wait()
    for u in range(NF):
        lo = up_ref[:, 256 * u : 256 * u + 128].astype(F32)
        hi = up_ref[:, 256 * u + 128 : 256 * u + 256].astype(F32)
        wg[zh, y, c, 512 + 16 * u : 528 + 16 * u] = jnp.concatenate([lo, hi], axis=0).astype(BF)
    for copy in inputs[1:4]:
        copy.wait()
    pl.semaphore_wait(barrier, len(peers))

    part = MAIN // (nx * nq)
    main, tail = pl.ds(0, MAIN), pl.ds(MAIN, ROWS - MAIN)
    oz = 1 - zh
    own, other = wg.at[zh, y, c], wg.at[oz, y, c]
    far = dev(zh=oz, zl=half)
    piece = rows((x * nq + half % nq) * part, part)
    far_main = gather(own.at[piece], own.at[piece], far)
    far_tail = gather(own.at[tail], own.at[tail], far)
    tails = [gather(own.at[tail], own.at[tail], to) for to in near_y.values()]
    to_core = [gather(own.at[tail], own.at[tail], sibling)]
    mains = [gather(own.at[main], own.at[main], to) for to in near_y.values()]
    mains_core = [gather(own.at[main], own.at[main], sibling)]
    for k, copy in zip(near_y, tails):
        copy.wait_recv()
        got = wg.at[zh, (y - k + NY) % NY, c, tail]
        to_core.append(gather(got, got, sibling))
    far_main.wait_recv()
    piece = rows((x * nq + q) * part, part)
    step = [
        gather(other.at[piece], other.at[piece], dev(zl=b * nq + (q + k) % nq))
        for k in range(1, nq)
    ]
    far_tail.wait_recv()
    tails = [gather(other.at[tail], other.at[tail], to) for to in near_y.values()]
    to_core.append(gather(other.at[tail], other.at[tail], sibling))
    for s in step:
        s.wait_recv()
    piece = rows(x * nq * part, nq * part)
    shares = {}
    for i in range(nx):
        for k in (1, 3, 2, 0):
            if i or k:
                shares[i, k] = gather(
                    other.at[piece], other.at[piece], dev(x=(x + i) % nx, y=(y + k) % NY)
                )
    for k, copy in zip(near_y, tails):
        copy.wait_recv()
        got = wg.at[oz, (y - k + NY) % NY, c, tail]
        to_core.append(gather(got, got, sibling))
    for k, copy in zip(near_y, mains):
        copy.wait_recv()
        got = wg.at[zh, (y - k + NY) % NY, c, main]
        mains_core.append(gather(got, got, sibling))

    for s in to_core:
        s.wait_recv()
    inputs[4].wait()
    emb = x_ref[...]
    proj = wg[:, :, :, MAIN:ROWS, :].reshape(feats, 128)
    compressed = mm(emb, proj, 0, 0).astype(BF)
    fm = mm(emb, compressed)
    centre = fm - jnp.mean(fm, axis=-1, keepdims=True)
    inv = lax.rsqrt(jnp.mean(centre * centre, axis=-1, keepdims=True) + 1e-05)
    normed = centre * inv
    nl[...] = normed.astype(BF)
    nlt[...] = normed.T.astype(BF)
    gn[...] = jnp.zeros_like(gn)
    inputs[5].wait()
    inputs[6].wait()

    for i in range(nx):
        for k in range(NY):
            if i or k:
                shares[i, k].wait_recv()
        got = wg.at[oz, :, c, rows(((x - i + nx) % nx) * nq * part, nq * part)]
        mains_core.append(gather(got, got, sibling))
    for s in mains_core:
        s.wait_recv()

    def hidden_units(izh, iy, ic):
        u = (izh * NY + iy) * NC + ic
        urows = rows(512 + 16 * u, 16)
        pieces = wg[:, :, :, urows, :].reshape(NF, 16, 128).astype(F32)
        up = jnp.concatenate(
            [pieces[:, 0:8].reshape(128, 128), pieces[:, 8:16].reshape(128, 128)], axis=1
        ).astype(BF)
        down = jnp.concatenate([wg[izh, iy, ic, 0:256], wg[izh, iy, ic, 256:512]], axis=1)
        cots = cot_ref[...]
        hidden = mm(nl[...], up)
        sig = 0.5 * jnp.tanh(0.5 * hidden) + 0.5
        act = (hidden * sig).astype(BF)
        gh = (mm(cots, down, 1, 1) * sig * (1.0 + hidden * (1.0 - sig))).astype(BF)
        gn[...] += mm(gh, up, 1, 1)
        gup = mm(nlt[...], gh)
        gup = jnp.concatenate(
            [gup[:, 0:128].reshape(NF, 8, 128), gup[:, 128:256].reshape(NF, 8, 128)], axis=1
        ).astype(BF)
        gg[:, :, :, urows, :] = gup.reshape(NZH, NY, NC, 16, 128)
        gdn = mm(act, cots, 0, 0).astype(BF)
        gg[izh, iy, ic, 0:256] = gdn[:, 0:128]
        gg[izh, iy, ic, 256:512] = gdn[:, 128:256]

    def core_copy(i):
        izh, iy = i // NY, i % NY
        down = pl.ds(0, 512)
        return remote(
            gg.at[izh, iy, 1 - c, down], rc.at[izh, iy, down], co_s, co_r, i, sibling
        )

    @pl.loop(0, NZH * NY)
    def _(i):
        hidden_units(i // NY, i % NY, 1 - c)
        core_copy(i).start()
        hidden_units(i // NY, i % NY, c)

    upper = pl.ds(512, MAIN - 512)
    r0 = [reduce(gg.at[:, :, 1 - c, upper], rc.at[:, :, upper], sibling)]
    for i in range(NZH * NY):
        core_copy(i).wait()
    r1a = []
    blk = 96
    for k in (1, 3, 2, 0):
        to = (y + k) % NY

        @pl.loop(0, CUT // blk)
        def _(i, to=to):
            r = rows(i * blk, blk)
            sa[to, :, r] = (gg[:, to, c, r].astype(F32) + rc[:, to, r].astype(F32)).astype(BF)

        if k:
            r1a.append(reduce(sa.at[to, :, 0:CUT], rya.at[k - 1], near_y[k]))

    gnorm = gn[...]
    gfm = inv * (
        gnorm
        - jnp.mean(gnorm, axis=-1, keepdims=True)
        - normed * jnp.mean(gnorm * normed, axis=-1, keepdims=True)
    )
    gfm = gfm.astype(BF)
    gcomp = mm(emb, gfm, 0, 0).astype(BF)
    gproj = mm(emb, gcomp).astype(BF)
    gg[:, :, :, MAIN:ROWS, :] = gproj.reshape(NZH, NY, NC, 16, 128)
    r0.append(reduce(gg.at[:, :, 1 - c, tail], rc.at[:, :, tail], sibling))
    for s in r0:
        s.wait_recv()
    r1b = []
    for k in [*range(1, nx), 0]:
        at = rows(CUT + ((x + k) % nx) * xb, xb)

        @pl.loop(0, NY)
        def _(i, at=at):
            sa[i, :, at] = (gg[:, i, c, at].astype(F32) + rc[:, i, at].astype(F32)).astype(BF)

        if k:
            r1b.append(reduce(sa.at[:, :, at], rxb.at[k - 1], near_x[k]))

    gemb = (mm(gfm, compressed, 1, 1) + mm(proj, gcomp, 1, 1)).astype(BF)

    row = lax.broadcasted_iota(jnp.int32, (feats, feats), 0)
    col = lax.broadcasted_iota(jnp.int32, (feats, feats), 1)
    across_f = jnp.broadcast_to(own_ref[...].astype(F32), (feats, feats))
    down_f = jnp.sum(jnp.where(row == col, across_f, 0.0), axis=1, keepdims=True)
    within = jnp.sum(
        jnp.where((across_f == down_f) & (row < col), 1.0, 0.0), axis=0, keepdims=True
    )
    owner = across_f[0:1]
    owner_x = jnp.floor(owner * (1.0 / nzl))
    place = (owner - owner_x * nzl) * zrows + owner_x * per + within
    perm = jnp.where(row.astype(F32) == place, 1.0, 0.0).astype(BF)
    av1[...] = mm(perm, gemb).astype(BF)
    a1 = []
    mine = rows(zl * zrows, zrows)
    for k in range(1, nzl):
        to = (zl + k) % nzl
        a1.append(exchange(av1.at[rows(to * zrows, zrows)], av2.at[mine], dev(zl=to)))
    av2[mine] = av1[mine]

    for s in r1a:
        s.wait_recv()
    r2 = []
    for k in [*range(1, nx), 0]:
        at = rows(((x + k) % nx) * xa, xa)
        t = sa[y, :, at].astype(F32)
        for j in range(NY - 1):
            t += rya[j, :, at].astype(F32)
        sba[:, at] = t.astype(BF)
        if k:
            r2.append(reduce(sba.at[:, at], rxa.at[k - 1], near_x[k]))
    for s in r1b:
        s.wait_recv()
    at = rows(CUT + x * xb, xb)
    for k in (1, 3, 2, 0):
        to = (y + k) % NY
        t = sa[to, :, at].astype(F32)
        for j in range(nx - 1):
            t += rxb[j, to].astype(F32)
        sbb[to] = t.astype(BF)
        if k:
            r2.append(reduce(sbb.at[to], ryb.at[k - 1], near_y[k]))
    for s in r2:
        s.wait_recv()
    t = sba[:, rows(x * xa, xa)].astype(F32)
    for j in range(nx - 1):
        t += rxa[j].astype(F32)
    sc[:, 0:xa] = t.astype(BF)
    t = sbb[y].astype(F32)
    for j in range(NY - 1):
        t += ryb[j].astype(F32)
    sc[:, xa:xp] = t.astype(BF)

    r3 = []
    for k in range(1, nq):
        to = (q + k) % nq
        r3.append(reduce(sc.at[:, rows(to * qp, qp)], rq.at[k - 1], dev(zl=b * nq + to)))
    for s in r3:
        s.wait_recv()
    t = sc[:, rows(q * qp, qp)].astype(F32)
    for j in range(nq - 1):
        t += rq[j].astype(F32)
    se[...] = t.astype(BF)

    r4 = []
    for k in range(NZH * nb - 1, 0, -1):
        h2, b2 = (zh + k // nb) % NZH, (b + k % nb) % nb
        r4.append(reduce(se.at[h2], rb.at[k - 1], dev(zh=h2, zl=b2 * nq + q)))

    for s in a1:
        s.wait_recv()
    r_z, r_x, r_k = col // zrows, (col % zrows) // per, col % per
    perm = jnp.where(row == r_x * (nzl * per) + r_z * per + r_k, 1.0, 0.0).astype(BF)
    av3[...] = mm(perm, av2[...]).astype(BF)
    a2 = []
    xrows = nzl * per
    mine = rows(x * xrows, xrows)
    for k in range(1, nx):
        to = (x + k) % nx
        a2.append(exchange(av3.at[rows(to * xrows, xrows)], av4.at[mine], near_x[k]))
    av4[mine] = av3[mine]

    for s in r4:
        s.wait_recv()
    t = se[zh].astype(F32)
    for j in range(NZH * nb - 1):
        t += rb[j].astype(F32)
    mine = rows(q * qp, qp)
    ox[x, mine] = t.astype(BF)

    ref = ox.at[x, mine]
    step = [reduce(ref, ref, dev(zl=b * nq + (q + k) % nq)) for k in range(1, nq)]
    for s in a2:
        s.wait_recv()
    owned_ref[...] = av4[...]
    for s in step:
        s.wait_recv()
    ref = ox.at[x, 0:xp]
    step = [reduce(ref, ref, to) for to in near_x.values()]
    for s in step:
        s.wait_recv()

    scale = 1.0 / (nx * nzl * NF)

    def unit(i):
        at = i * 16
        px, at = (at // xa, at % xa) if at < CUT else ((at - CUT) // xb, xa + (at - CUT) % xb)
        return ox[px, at : at + 16, :].astype(F32) * scale

    for i in range(16):
        gdn_ref[16 * i : 16 * i + 16, 0:128] = unit(i)
        gdn_ref[16 * i : 16 * i + 16, 128:256] = unit(16 + i)
        t = unit(32 + i)
        gup_ref[:, 256 * i : 256 * i + 128] = t[0:8]
        gup_ref[:, 256 * i + 128 : 256 * i + 256] = t[8:16]
    gproj_ref[...] = unit(48)
    for s in pending:
        s.wait_send()


def per_device(split, embeddings, cotangent, owners, projection, up_weight, down_weight):
    nx, nzl, nq = split
    nb = nzl // nq
    feats, width = embeddings.shape[1:]
    xa = CUT // nx
    xb = 16 * -(-(ROWS - CUT) // (16 * nx))
    qp = 16 * -(-(xa + xb) // (16 * nq))
    padded = CUT + nx * xb
    n_ag = 20 + (nq - 1) + (nx * NY - 1) + 3 + nx
    n_rs = 2 + 2 * (NY - 1) + 3 * (nx - 1) + 2 * (nq - 1) + (NZH * nb - 1)
    n_aa = nzl - 1 + nx - 1
    vmem = pl.BlockSpec(memory_space=pltpu.VMEM)
    return pl.pallas_call(
        functools.partial(kernel, split),
        out_shape=(
            jax.ShapeDtypeStruct((feats, width), BF),
            jax.ShapeDtypeStruct(projection.shape, F32),
            jax.ShapeDtypeStruct(up_weight.shape, F32),
            jax.ShapeDtypeStruct(down_weight.shape, F32),
        ),
        in_specs=[pl.BlockSpec(memory_space=pl.ANY)] * 6,
        out_specs=(vmem,) * 4,
        scratch_shapes=[
            pltpu.VMEM((feats, width), BF),
            pltpu.VMEM((feats, width), BF),
            pltpu.VMEM(owners.shape, jnp.int32),
            pltpu.VMEM(up_weight.shape, BF),
            pltpu.VMEM((NZH, NY, NC, ROWS, 128), BF),
            pltpu.VMEM((NZH, NY, NC, padded, 128), BF),
            pltpu.VMEM((NZH, NY, padded, 128), BF),
            pltpu.VMEM((NY, NZH, padded, 128), BF),
            pltpu.VMEM((NY - 1, NZH, CUT, 128), BF),
            pltpu.VMEM((NZH, CUT, 128), BF),
            pltpu.VMEM((nx - 1, NZH, xa, 128), BF),
            pltpu.VMEM((nx - 1, NY, NZH, xb, 128), BF),
            pltpu.VMEM((NY, NZH, xb, 128), BF),
            pltpu.VMEM((NY - 1, NZH, xb, 128), BF),
            pltpu.VMEM((NZH, nq * qp, 128), BF),
            pltpu.VMEM((nq - 1, NZH, qp, 128), BF),
            pltpu.VMEM((NZH, qp, 128), BF),
            pltpu.VMEM((NZH * nb - 1, qp, 128), BF),
            pltpu.VMEM((nx, nq * qp, 128), BF),
            pltpu.VMEM((feats, 128), BF),
            pltpu.VMEM((128, feats), BF),
            pltpu.VMEM((feats, 128), F32),
            pltpu.VMEM((feats, width), BF),
            pltpu.VMEM((feats, width), BF),
            pltpu.VMEM((feats, width), BF),
            pltpu.VMEM((feats, width), BF),
            pltpu.SemaphoreType.DMA((7,)),
            pltpu.SemaphoreType.DMA((n_ag,)),
            pltpu.SemaphoreType.DMA((n_ag,)),
            pltpu.SemaphoreType.DMA((NZH * NY,)),
            pltpu.SemaphoreType.DMA((NZH * NY,)),
            pltpu.SemaphoreType.DMA((n_rs,)),
            pltpu.SemaphoreType.DMA((n_rs,)),
            pltpu.SemaphoreType.DMA((n_aa,)),
            pltpu.SemaphoreType.DMA((n_aa,)),
        ],
        compiler_params=pltpu.CompilerParams(
            collective_id=0, has_side_effects=True, vmem_limit_bytes=48 * 1024 * 1024
        ),
        name="layer_backward",
    )(embeddings, cotangent, owners, projection, up_weight, down_weight)


def solution(mesh):
    return jax.shard_map(
        functools.partial(per_device, SPLITS[mesh.shape["dp"]]),
        mesh=mesh,
        in_specs=(
            P(("dp", "fsdp"), None, None),
            P(("dp", "fsdp"), None, None),
            P(("dp", "fsdp"), None),
            P("fsdp", None),
            P("fsdp", None),
            P("fsdp", None),
        ),
        out_specs=(P(("dp", "fsdp"), None), P("fsdp", None), P("fsdp", None), P("fsdp", None)),
        check_vma=False,
    )
```

```python
import functools

import jax
import jax.numpy as jnp
from jax import lax
from jax.experimental import pallas as pl
from jax.experimental.pallas import tpu as pltpu
from jax.sharding import PartitionSpec as P

BF = jnp.bfloat16
F32 = jnp.float32
SPLITS = {64: (4, 16, 4), 4: (2, 2, 2), 8: (2, 4, 2)}
NZH, NY, NC = 2, 4, 2
NF = NZH * NY * NC
MAIN, ROWS, CUT = 768, 784, 512


def mm(a, b, ca=1, cb=0):
    return lax.dot_general(a, b, (((ca,), (cb,)), ((), ())), preferred_element_type=F32)


def kernel(
    split, x_hbm, cot_hbm, own_hbm, proj_hbm, up_hbm, dn_hbm,
    owned_ref, gproj_ref, gup_ref, gdn_ref,
    x_ref, cot_ref, own_ref, up_ref,
    wg, gg, rc, sa, rya, sba, rxa, rxb, sbb, ryb, ryt, st, rxt, sc, rq, se, rb, ox,
    nl, nlt, gn, av1, av2, av3, av4,
    in_s, ag_s, ag_r, co_s, co_r, rs_s, rs_r, aa_s, aa_r,
):
    nx, nzl, nq = split
    nb = nzl // nq
    feats = x_ref.shape[0]
    xa, xb = rxa.shape[2], rxb.shape[3]
    xp, qp = xa + xb, se.shape[1]
    pq = xp // nq
    zrows = feats // nzl
    per = zrows // nx
    dp, fs = lax.axis_index("dp"), lax.axis_index("fsdp")
    x, zl = dp // nzl, dp % nzl
    zh, y, c = fs // (NY * NC), (fs // NC) % NY, fs % NC
    q, b = zl % nq, zl // nq

    def dev(x=x, zl=zl, zh=zh, y=y, c=c):
        return {"dp": x * nzl + zl, "fsdp": (zh * NY + y) * NC + c}

    pending = []

    def remote(src, dst, ssem, rsem, i, to):
        return pltpu.make_async_remote_copy(
            src_ref=src, dst_ref=dst, send_sem=ssem.at[i], recv_sem=rsem.at[i],
            device_id=to, device_id_type=pl.DeviceIdType.MESH,
        )

    def sender(ssem, rsem):
        count = [0]

        def send(src, dst, to):
            copy = remote(src, dst, ssem, rsem, count[0], to)
            count[0] += 1
            copy.start()
            pending.append(copy)
            return copy

        return send

    def rows(start, size):
        return pl.ds(pl.multiple_of(start, 16), size)

    gather, reduce, exchange = sender(ag_s, ag_r), sender(rs_s, rs_r), sender(aa_s, aa_r)
    sibling = dev(c=1 - c)
    near_y = {k: dev(y=(y + k) % NY) for k in (1, 3, 2)}
    near_x = {k: dev(x=(x + k) % nx) for k in range(1, nx)}

    barrier = pltpu.get_barrier_semaphore()
    peers = [sibling]
    peers += [
        dev(x=(x + i) % nx, y=(y + k) % NY) for i in range(nx) for k in range(NY) if i or k
    ]
    peers += [dev(zl=(zl + k) % nzl) for k in range(1, nzl)]
    peers += [dev(zh=1 - zh, zl=((b + k) % nb) * nq + q) for k in range(nb)]
    half = ((zl + nzl // 2) % nzl)
    if (nzl // 2) % nq:
        peers.append(dev(zh=1 - zh, zl=half))
    for p in peers:
        pl.semaphore_signal(barrier, inc=1, device_id=p, device_id_type=pl.DeviceIdType.MESH)

    inputs = [
        pltpu.make_async_copy(src, dst, in_s.at[i])
        for i, (src, dst) in enumerate(
            (
                (up_hbm, up_ref),
                (proj_hbm, wg.at[zh, y, c, MAIN:ROWS]),
                (dn_hbm.at[:, 0:128], wg.at[zh, y, c, 0:256]),
                (dn_hbm.at[:, 128:256], wg.at[zh, y, c, 256:512]),
                (x_hbm.at[0], x_ref),
                (own_hbm, own_ref),
                (cot_hbm.at[0], cot_ref),
            )
        )
    ]
    for copy in inputs:
        copy.start()
    inputs[0].wait()
    for u in range(NF):
        lo = up_ref[:, 256 * u : 256 * u + 128].astype(F32)
        hi = up_ref[:, 256 * u + 128 : 256 * u + 256].astype(F32)
        wg[zh, y, c, 512 + 16 * u : 528 + 16 * u] = jnp.concatenate([lo, hi], axis=0).astype(BF)
    for copy in inputs[1:4]:
        copy.wait()
    pl.semaphore_wait(barrier, len(peers))

    parts = ((CUT, (MAIN - CUT) // (nx * nq)), (0, CUT // (nx * nq)))
    main, tail = pl.ds(0, MAIN), pl.ds(MAIN, ROWS - MAIN)
    oz = 1 - zh
    own, other = wg.at[zh, y, c], wg.at[oz, y, c]
    far = dev(zh=oz, zl=half)

    def swap(ref, to):
        return gather(ref, ref, to)

    far_main = []
    for base, size in parts:
        far_main.append(swap(own.at[rows(base + (x * nq + half % nq) * size, size)], far))
        if base:
            far_tail = swap(own.at[tail], far)
    tails = [swap(own.at[tail], to) for to in near_y.values()]
    to_core = [swap(own.at[tail], sibling)]
    mains = [swap(own.at[main], to) for to in near_y.values()]
    mains_core = [swap(own.at[main], sibling)]
    for k, copy in zip(near_y, tails):
        copy.wait_recv()
        to_core.append(swap(wg.at[zh, (y - k + NY) % NY, c, tail], sibling))
    steps = []
    for n, (base, size) in enumerate(parts):
        far_main[n].wait_recv()
        piece = rows(base + (x * nq + q) * size, size)
        steps.append(
            [swap(other.at[piece], dev(zl=b * nq + (q + k) % nq)) for k in range(1, nq)]
        )
        if n == 0:
            far_tail.wait_recv()
            tails = [swap(other.at[tail], to) for to in near_y.values()]
            to_core.append(swap(other.at[tail], sibling))
    shares = {}
    for n, (base, size) in enumerate(parts):
        for s in steps[n]:
            s.wait_recv()
        piece = rows(base + x * nq * size, nq * size)
        for i in range(nx):
            for k in (1, 3, 2, 0):
                if i or k:
                    shares[n, i, k] = swap(
                        other.at[piece], dev(x=(x + i) % nx, y=(y + k) % NY)
                    )
    for k, copy in zip(near_y, tails):
        copy.wait_recv()
        to_core.append(swap(wg.at[oz, (y - k + NY) % NY, c, tail], sibling))
    for k, copy in zip(near_y, mains):
        copy.wait_recv()
        mains_core.append(swap(wg.at[zh, (y - k + NY) % NY, c, main], sibling))

    def to_sibling(n, i):
        base, size = parts[n]
        for k in range(NY):
            if i or k:
                shares[n, i, k].wait_recv()
        at = rows(base + ((x - i + nx) % nx) * nq * size, nq * size)
        return swap(wg.at[oz, :, c, at], sibling)

    for s in to_core:
        s.wait_recv()
    inputs[4].wait()
    emb = x_ref[...]
    proj = wg[:, :, :, MAIN:ROWS, :].reshape(feats, 128)
    compressed = mm(emb, proj, 0, 0).astype(BF)
    fm = mm(emb, compressed)
    centre = fm - jnp.mean(fm, axis=-1, keepdims=True)
    inv = lax.rsqrt(jnp.mean(centre * centre, axis=-1, keepdims=True) + 1e-05)
    normed = centre * inv
    nl[...] = normed.astype(BF)
    nlt[...] = normed.T.astype(BF)
    gn[...] = jnp.zeros_like(gn)
    inputs[5].wait()
    inputs[6].wait()

    mains_core += [to_sibling(0, i) for i in range(nx)]
    for s in mains_core:
        s.wait_recv()

    def hidden_units(izh, iy, ic):
        u = (izh * NY + iy) * NC + ic
        urows = rows(512 + 16 * u, 16)
        pieces = wg[:, :, :, urows, :].reshape(NF, 16, 128).astype(F32)
        up = jnp.concatenate(
            [pieces[:, 0:8].reshape(128, 128), pieces[:, 8:16].reshape(128, 128)], axis=1
        ).astype(BF)
        down = jnp.concatenate([wg[izh, iy, ic, 0:256], wg[izh, iy, ic, 256:512]], axis=1)
        cots = cot_ref[...]
        hidden = mm(nl[...], up)
        sig = 0.5 * jnp.tanh(0.5 * hidden) + 0.5
        act = (hidden * sig).astype(BF)
        gh = (mm(cots, down, 1, 1) * sig * (1.0 + hidden * (1.0 - sig))).astype(BF)
        gn[...] += mm(gh, up, 1, 1)
        gup = mm(nlt[...], gh)
        gup = jnp.concatenate(
            [gup[:, 0:128].reshape(NF, 8, 128), gup[:, 128:256].reshape(NF, 8, 128)], axis=1
        ).astype(BF)
        gg[:, :, :, urows, :] = gup.reshape(NZH, NY, NC, 16, 128)
        gdn = mm(act, cots, 0, 0).astype(BF)
        gg[izh, iy, ic, 0:256] = gdn[:, 0:128]
        gg[izh, iy, ic, 256:512] = gdn[:, 128:256]

    down = pl.ds(0, CUT)

    def core_copy(h, i):
        izh = (zh + h) % NZH
        return remote(
            gg.at[izh, i, 1 - c, down], rc.at[izh, i, down], co_s, co_r, h * NY + i, sibling
        )

    def hidden_loop(h, first, last):
        @pl.loop(first, last)
        def _(i):
            izh = (zh + h) % NZH
            hidden_units(izh, i, 1 - c)
            core_copy(h, i).start()
            hidden_units(izh, i, c)

    r1a = []

    def down_sums(h):
        izh = (zh + h) % NZH
        for i in range(NY):
            core_copy(h, i).wait()
        for k in (1, 3, 2, 0):
            to = (y + k) % NY

            @pl.loop(0, CUT // 128)
            def _(i, to=to):
                r = rows(i * 128, 128)
                sa[to, izh, r] = (
                    gg[izh, to, c, r].astype(F32) + rc[izh, to, r].astype(F32)
                ).astype(BF)

            if k:
                r1a.append(reduce(sa.at[to, izh, down], rya.at[k - 1, izh], near_y[k]))

    hidden_loop(0, 0, 2)
    late = [to_sibling(1, i) for i in range(nx // 2)]
    hidden_loop(0, 2, NY)
    late += [to_sibling(1, i) for i in range(nx // 2, nx)]
    down_sums(0)
    for s in late:
        s.wait_recv()
    hidden_loop(1, 0, NY)
    upper = pl.ds(CUT, MAIN - CUT)
    r0 = reduce(gg.at[:, :, 1 - c, upper], rc.at[:, :, upper], sibling)
    down_sums(1)
    r0.wait_recv()
    r1b = []
    for k in [*range(1, nx), 0]:
        at = rows(CUT + ((x + k) % nx) * xb, xb)

        @pl.loop(0, NY)
        def _(i, at=at):
            sa[i, :, at] = (gg[:, i, c, at].astype(F32) + rc[:, i, at].astype(F32)).astype(BF)

        if k:
            r1b.append(reduce(sa.at[:, :, at], rxb.at[k - 1], near_x[k]))

    gnorm = gn[...]
    gfm = inv * (
        gnorm
        - jnp.mean(gnorm, axis=-1, keepdims=True)
        - normed * jnp.mean(gnorm * normed, axis=-1, keepdims=True)
    )
    gfm = gfm.astype(BF)
    gcomp = mm(emb, gfm, 0, 0).astype(BF)
    gproj = mm(emb, gcomp).astype(BF)
    gg[:, :, :, MAIN:ROWS, :] = gproj.reshape(NZH, NY, NC, 16, 128)
    r0 = reduce(gg.at[:, :, 1 - c, tail], rc.at[:, :, tail], sibling)
    gemb = (mm(gfm, compressed, 1, 1) + mm(proj, gcomp, 1, 1)).astype(BF)

    row = lax.broadcasted_iota(jnp.int32, (feats, feats), 0)
    col = lax.broadcasted_iota(jnp.int32, (feats, feats), 1)
    across_f = jnp.broadcast_to(own_ref[...].astype(F32), (feats, feats))
    down_f = jnp.sum(jnp.where(row == col, across_f, 0.0), axis=1, keepdims=True)
    within = jnp.sum(
        jnp.where((across_f == down_f) & (row < col), 1.0, 0.0), axis=0, keepdims=True
    )
    owner = across_f[0:1]
    owner_x = jnp.floor(owner * (1.0 / nzl))
    place = (owner - owner_x * nzl) * zrows + owner_x * per + within
    perm = jnp.where(row.astype(F32) == place, 1.0, 0.0).astype(BF)
    av1[...] = mm(perm, gemb).astype(BF)
    a1 = []
    mine = rows(zl * zrows, zrows)
    for k in range(1, nzl):
        to = (zl + k) % nzl
        a1.append(exchange(av1.at[rows(to * zrows, zrows)], av2.at[mine], dev(zl=to)))
    av2[mine] = av1[mine]

    r0.wait_recv()
    r1t = []
    for k in (1, 3, 2, 0):
        to = (y + k) % NY
        sa[to, :, tail] = (gg[:, to, c, tail].astype(F32) + rc[:, to, tail].astype(F32)).astype(BF)
        if k:
            r1t.append(reduce(sa.at[to, :, tail], ryt.at[k - 1], near_y[k]))

    for s in r1a:
        s.wait_recv()
    r2 = []
    for k in [*range(1, nx), 0]:
        at = rows(((x + k) % nx) * xa, xa)
        t = sa[y, :, at].astype(F32)
        for j in range(NY - 1):
            t += rya[j, :, at].astype(F32)
        sba[:, at] = t.astype(BF)
        if k:
            r2.append(reduce(sba.at[:, at], rxa.at[k - 1], near_x[k]))
    for s in r1b:
        s.wait_recv()
    at = rows(CUT + x * xb, xb)
    for k in (1, 3, 2, 0):
        to = (y + k) % NY
        t = sa[to, :, at].astype(F32)
        for j in range(nx - 1):
            t += rxb[j, to].astype(F32)
        sbb[to] = t.astype(BF)
        if k:
            r2.append(reduce(sbb.at[to], ryb.at[k - 1], near_y[k]))
    for s in r1t:
        s.wait_recv()
    t = sa[y, :, tail].astype(F32)
    for j in range(NY - 1):
        t += ryt[j].astype(F32)
    st[...] = t.astype(BF)
    r2 += [reduce(st, rxt.at[k - 1], near_x[k]) for k in range(1, nx)]
    for s in r2:
        s.wait_recv()
    ta = sba[:, rows(x * xa, xa)].astype(F32)
    for j in range(nx - 1):
        ta += rxa[j].astype(F32)
    tb = sbb[y].astype(F32)
    for j in range(NY - 1):
        tb += ryb[j].astype(F32)
    tt = st[...].astype(F32)
    for j in range(nx - 1):
        tt += rxt[j].astype(F32)
    t = jnp.concatenate([ta, tb], axis=1)
    for j in range(nq):
        sc[:, j] = jnp.concatenate([t[:, j * pq : (j + 1) * pq], tt], axis=1).astype(BF)

    r3 = []
    for k in range(1, nq):
        to = (q + k) % nq
        r3.append(reduce(sc.at[:, to], rq.at[k - 1], dev(zl=b * nq + to)))
    for s in r3:
        s.wait_recv()
    t = sc[:, q].astype(F32)
    for j in range(nq - 1):
        t += rq[j].astype(F32)
    se[...] = t.astype(BF)

    r4 = []
    for k in range(NZH * nb - 1, 0, -1):
        h2, b2 = (zh + k // nb) % NZH, (b + k % nb) % nb
        r4.append(reduce(se.at[h2], rb.at[k - 1], dev(zh=h2, zl=b2 * nq + q)))

    for s in a1:
        s.wait_recv()
    r_z, r_x, r_k = col // zrows, (col % zrows) // per, col % per
    perm = jnp.where(row == r_x * (nzl * per) + r_z * per + r_k, 1.0, 0.0).astype(BF)
    av3[...] = mm(perm, av2[...]).astype(BF)
    a2 = []
    xrows = nzl * per
    mine = rows(x * xrows, xrows)
    for k in range(1, nx):
        to = (x + k) % nx
        a2.append(exchange(av3.at[rows(to * xrows, xrows)], av4.at[mine], near_x[k]))
    av4[mine] = av3[mine]

    for s in r4:
        s.wait_recv()
    t = se[zh].astype(F32)
    for j in range(NZH * nb - 1):
        t += rb[j].astype(F32)
    t_proj = t[pq:qp]
    ox[x, q] = t[0:pq].astype(BF)

    step = [reduce(ox.at[x, q], ox.at[x, q], dev(zl=b * nq + (q + k) % nq)) for k in range(1, nq)]
    last = [reduce(ox.at[x, q], ox.at[x, q], to) for to in near_x.values()]
    for k, copy in enumerate(step, 1):
        copy.wait_recv()
        ref = ox.at[x, (q - k + nq) % nq]
        last += [reduce(ref, ref, to) for to in near_x.values()]
    for s in a2:
        s.wait_recv()
    owned_ref[...] = av4[...]
    for s in last:
        s.wait_recv()

    scale = 1.0 / (nx * nzl * NF)

    def unit(i):
        at = i * 16
        px, at = (at // xa, at % xa) if at < CUT else ((at - CUT) // xb, xa + (at - CUT) % xb)
        return ox[px, at // pq, at % pq : at % pq + 16, :].astype(F32) * scale

    for i in range(16):
        gdn_ref[16 * i : 16 * i + 16, 0:128] = unit(i)
        gdn_ref[16 * i : 16 * i + 16, 128:256] = unit(16 + i)
        t = unit(32 + i)
        gup_ref[:, 256 * i : 256 * i + 128] = t[0:8]
        gup_ref[:, 256 * i + 128 : 256 * i + 256] = t[8:16]
    gproj_ref[...] = t_proj * scale
    for s in pending:
        s.wait_send()


def per_device(split, embeddings, cotangent, owners, projection, up_weight, down_weight):
    nx, nzl, nq = split
    nb = nzl // nq
    feats, width = embeddings.shape[1:]
    xa = CUT // nx
    xb = (MAIN - CUT) // nx
    pq = (xa + xb) // nq
    qp = pq + ROWS - MAIN
    n_ag = 21 + 2 * (nq - 1) + 2 * (nx * NY - 1) + 3 + 2 * nx
    n_rs = 2 + 4 * (NY - 1) + 3 * (nx - 1) + 2 * (nq - 1) + (NZH * nb - 1) + nq * (nx - 1) + 3
    n_aa = nzl - 1 + nx - 1
    vmem = pl.BlockSpec(memory_space=pltpu.VMEM)
    return pl.pallas_call(
        functools.partial(kernel, split),
        out_shape=(
            jax.ShapeDtypeStruct((feats, width), BF),
            jax.ShapeDtypeStruct(projection.shape, F32),
            jax.ShapeDtypeStruct(up_weight.shape, F32),
            jax.ShapeDtypeStruct(down_weight.shape, F32),
        ),
        in_specs=[pl.BlockSpec(memory_space=pl.ANY)] * 6,
        out_specs=(vmem,) * 4,
        scratch_shapes=[
            pltpu.VMEM((feats, width), BF),
            pltpu.VMEM((feats, width), BF),
            pltpu.VMEM(owners.shape, jnp.int32),
            pltpu.VMEM(up_weight.shape, BF),
            pltpu.VMEM((NZH, NY, NC, ROWS, 128), BF),
            pltpu.VMEM((NZH, NY, NC, ROWS, 128), BF),
            pltpu.VMEM((NZH, NY, ROWS, 128), BF),
            pltpu.VMEM((NY, NZH, ROWS, 128), BF),
            pltpu.VMEM((NY - 1, NZH, CUT, 128), BF),
            pltpu.VMEM((NZH, CUT, 128), BF),
            pltpu.VMEM((nx - 1, NZH, xa, 128), BF),
            pltpu.VMEM((nx - 1, NY, NZH, xb, 128), BF),
            pltpu.VMEM((NY, NZH, xb, 128), BF),
            pltpu.VMEM((NY - 1, NZH, xb, 128), BF),
            pltpu.VMEM((NY - 1, NZH, ROWS - MAIN, 128), BF),
            pltpu.VMEM((NZH, ROWS - MAIN, 128), BF),
            pltpu.VMEM((nx - 1, NZH, ROWS - MAIN, 128), BF),
            pltpu.VMEM((NZH, nq, qp, 128), BF),
            pltpu.VMEM((nq - 1, NZH, qp, 128), BF),
            pltpu.VMEM((NZH, qp, 128), BF),
            pltpu.VMEM((NZH * nb - 1, qp, 128), BF),
            pltpu.VMEM((nx, nq, pq, 128), BF),
            pltpu.VMEM((feats, 128), BF),
            pltpu.VMEM((128, feats), BF),
            pltpu.VMEM((feats, 128), F32),
            pltpu.VMEM((feats, width), BF),
            pltpu.VMEM((feats, width), BF),
            pltpu.VMEM((feats, width), BF),
            pltpu.VMEM((feats, width), BF),
            pltpu.SemaphoreType.DMA((7,)),
            pltpu.SemaphoreType.DMA((n_ag,)),
            pltpu.SemaphoreType.DMA((n_ag,)),
            pltpu.SemaphoreType.DMA((NZH * NY,)),
            pltpu.SemaphoreType.DMA((NZH * NY,)),
            pltpu.SemaphoreType.DMA((n_rs,)),
            pltpu.SemaphoreType.DMA((n_rs,)),
            pltpu.SemaphoreType.DMA((n_aa,)),
            pltpu.SemaphoreType.DMA((n_aa,)),
        ],
        compiler_params=pltpu.CompilerParams(
            collective_id=0, has_side_effects=True, vmem_limit_bytes=56 * 1024 * 1024
        ),
        name="layer_backward",
    )(embeddings, cotangent, owners, projection, up_weight, down_weight)


def solution(mesh):
    return jax.shard_map(
        functools.partial(per_device, SPLITS[mesh.shape["dp"]]),
        mesh=mesh,
        in_specs=(
            P(("dp", "fsdp"), None, None),
            P(("dp", "fsdp"), None, None),
            P(("dp", "fsdp"), None),
            P("fsdp", None),
            P("fsdp", None),
            P("fsdp", None),
        ),
        out_specs=(P(("dp", "fsdp"), None), P("fsdp", None), P("fsdp", None), P("fsdp", None)),
        check_vma=False,
    )
```

```python
import functools

import jax
import jax.numpy as jnp
from jax import lax
from jax.experimental import pallas as pl
from jax.experimental.pallas import tpu as pltpu
from jax.sharding import PartitionSpec as P

BF = jnp.bfloat16
F32 = jnp.float32
SPLITS = {64: (4, 16, 4), 4: (2, 2, 2), 8: (2, 4, 2)}
NZH, NY, NC = 2, 4, 2
NF = NZH * NY * NC
MAIN, ROWS, CUT = 768, 784, 512


def mm(a, b, ca=1, cb=0):
    return lax.dot_general(a, b, (((ca,), (cb,)), ((), ())), preferred_element_type=F32)


def kernel(
    split, x_hbm, cot_hbm, own_hbm, proj_hbm, up_hbm, dn_hbm,
    owned_ref, gproj_ref, gup_ref, gdn_ref,
    x_ref, cot_ref, own_ref, up_ref,
    wg, gg, rc, sa, rya, sba, rxa, rxb, sbb, ryb, ryt, st, rxt, sc, rq, se, rb, ox,
    nl, nlt, gn, av1, av2, av3, av4,
    in_s, ag_s, ag_r, co_s, co_r, rs_s, rs_r, aa_s, aa_r, met,
):
    nx, nzl, nq = split
    nb = nzl // nq
    feats = x_ref.shape[0]
    xa, xb = rxa.shape[2], rxb.shape[3]
    xp, qp = xa + xb, se.shape[1]
    pq = xp // nq
    zrows = feats // nzl
    per = zrows // nx
    dp, fs = lax.axis_index("dp"), lax.axis_index("fsdp")
    x, zl = dp // nzl, dp % nzl
    zh, y, c = fs // (NY * NC), (fs // NC) % NY, fs % NC
    q, b = zl % nq, zl // nq

    def dev(x=x, zl=zl, zh=zh, y=y, c=c):
        return {"dp": x * nzl + zl, "fsdp": (zh * NY + y) * NC + c}

    pending = []

    def remote(src, dst, ssem, rsem, i, to):
        return pltpu.make_async_remote_copy(
            src_ref=src, dst_ref=dst, send_sem=ssem.at[i], recv_sem=rsem.at[i],
            device_id=to, device_id_type=pl.DeviceIdType.MESH,
        )

    def sender(ssem, rsem):
        count = [0]

        def send(src, dst, to):
            copy = remote(src, dst, ssem, rsem, count[0], to)
            count[0] += 1
            copy.start()
            pending.append(copy)
            return copy

        return send

    def rows(start, size):
        return pl.ds(pl.multiple_of(start, 16), size)

    gather, reduce, exchange = sender(ag_s, ag_r), sender(rs_s, rs_r), sender(aa_s, aa_r)
    sibling = dev(c=1 - c)
    near_y = {k: dev(y=(y + k) % NY) for k in (1, 3, 2)}
    near_x = {k: dev(x=(x + k) % nx) for k in range(1, nx)}

    barrier = pltpu.get_barrier_semaphore()
    peers = [sibling]
    peers += [
        dev(x=(x + i) % nx, y=(y + k) % NY) for i in range(nx) for k in range(NY) if i or k
    ]
    peers += [dev(zl=b * nq + (q + k) % nq) for k in range(1, nq)]
    m, nm = zh * nb + b, NZH * nb

    def ring(k):
        to = (m + k) % nm
        return dev(zh=to // nb, zl=(to % nb) * nq + q)

    peers += [ring(k) for k in range(1, nm) if min(k, nm - k) <= 2]
    half = (zl + nzl // 2) % nzl
    if (nzl // 2) % nq:
        peers.append(dev(zh=1 - zh, zl=half))

    def tell(i, to):
        pl.semaphore_signal(met.at[i], inc=1, device_id=to, device_id_type=pl.DeviceIdType.MESH)

    for p in peers:
        pl.semaphore_signal(barrier, inc=1, device_id=p, device_id_type=pl.DeviceIdType.MESH)

    inputs = [
        pltpu.make_async_copy(src, dst, in_s.at[i])
        for i, (src, dst) in enumerate(
            (
                (up_hbm, up_ref),
                (proj_hbm, wg.at[zh, y, c, MAIN:ROWS]),
                (dn_hbm.at[:, 0:128], wg.at[zh, y, c, 0:256]),
                (dn_hbm.at[:, 128:256], wg.at[zh, y, c, 256:512]),
                (x_hbm.at[0], x_ref),
                (own_hbm, own_ref),
                (cot_hbm.at[0], cot_ref),
            )
        )
    ]
    for copy in inputs:
        copy.start()
    inputs[0].wait()
    for u in range(NF):
        lo = up_ref[:, 256 * u : 256 * u + 128].astype(F32)
        hi = up_ref[:, 256 * u + 128 : 256 * u + 256].astype(F32)
        wg[zh, y, c, 512 + 16 * u : 528 + 16 * u] = jnp.concatenate([lo, hi], axis=0).astype(BF)
    for copy in inputs[1:4]:
        copy.wait()
    pl.semaphore_wait(barrier, len(peers))
    if nm > 5:
        tell(0, ring(2))
        tell(0, ring(nm - 2))

    parts = ((CUT, (MAIN - CUT) // nx), (0, CUT // nx))
    main, tail = pl.ds(0, MAIN), pl.ds(MAIN, ROWS - MAIN)
    oz = 1 - zh
    own, other = wg.at[zh, y, c], wg.at[oz, y, c]
    far = dev(zh=oz, zl=half)

    def swap(ref, to):
        return gather(ref, ref, to)

    far_main = []
    for base, size in parts:
        far_main.append(swap(own.at[rows(base + x * size, size)], far))
        if base:
            far_tail = swap(own.at[tail], far)
    tails = [swap(own.at[tail], to) for to in near_y.values()]
    to_core = [swap(own.at[tail], sibling)]
    mains = [swap(own.at[main], to) for to in near_y.values()]
    mains_core = [swap(own.at[main], sibling)]
    for k, copy in zip(near_y, tails):
        copy.wait_recv()
        to_core.append(swap(wg.at[zh, (y - k + NY) % NY, c, tail], sibling))
    shares = {}
    for n, (base, size) in enumerate(parts):
        far_main[n].wait_recv()
        piece = rows(base + x * size, size)
        for i in range(nx):
            for k in (1, 3, 2, 0):
                if i or k:
                    shares[n, i, k] = swap(
                        other.at[piece], dev(x=(x + i) % nx, y=(y + k) % NY)
                    )
        if n == 0:
            far_tail.wait_recv()
            tails = [swap(other.at[tail], to) for to in near_y.values()]
            to_core.append(swap(other.at[tail], sibling))
    for k, copy in zip(near_y, tails):
        copy.wait_recv()
        to_core.append(swap(wg.at[oz, (y - k + NY) % NY, c, tail], sibling))
    for k, copy in zip(near_y, mains):
        copy.wait_recv()
        mains_core.append(swap(wg.at[zh, (y - k + NY) % NY, c, main], sibling))

    if nm > 5:
        pl.semaphore_wait(met.at[0], 2)
        for k in range(1, nq):
            tell(1, dev(zl=b * nq + (q + k) % nq))

    def to_sibling(n, i):
        base, size = parts[n]
        for k in range(NY):
            if i or k:
                shares[n, i, k].wait_recv()
        at = rows(base + ((x - i + nx) % nx) * size, size)
        return swap(wg.at[oz, :, c, at], sibling)

    for s in to_core:
        s.wait_recv()
    inputs[4].wait()
    emb = x_ref[...]
    proj = wg[:, :, :, MAIN:ROWS, :].reshape(feats, 128)
    compressed = mm(emb, proj, 0, 0).astype(BF)
    fm = mm(emb, compressed)
    centre = fm - jnp.mean(fm, axis=-1, keepdims=True)
    inv = lax.rsqrt(jnp.mean(centre * centre, axis=-1, keepdims=True) + 1e-05)
    normed = centre * inv
    nl[...] = normed.astype(BF)
    nlt[...] = normed.T.astype(BF)
    gn[...] = jnp.zeros_like(gn)
    inputs[5].wait()
    inputs[6].wait()

    mains_core += [to_sibling(0, i) for i in range(nx)]
    for s in mains_core:
        s.wait_recv()

    def hidden_units(izh, iy):
        cores = (1 - c, c)
        at = [rows(512 + 16 * ((izh * NY + iy) * NC + ic), 16) for ic in cores]
        pieces = [wg[:, :, :, r, :].reshape(NF, 16, 128).astype(F32) for r in at]
        up = jnp.concatenate(
            [p[:, e : e + 8].reshape(128, 128) for p in pieces for e in (0, 8)], axis=1
        ).astype(BF)
        downs = jnp.concatenate(
            [
                jnp.concatenate([wg[izh, iy, ic, 0:256], wg[izh, iy, ic, 256:512]], axis=1)
                for ic in cores
            ],
            axis=0,
        )
        cots = cot_ref[...]
        hidden = mm(nl[...], up)
        sig = 0.5 * jnp.tanh(0.5 * hidden) + 0.5
        act = (hidden * sig).astype(BF)
        gh = (mm(cots, downs, 1, 1) * sig * (1.0 + hidden * (1.0 - sig))).astype(BF)
        gdn = mm(act, cots, 0, 0).astype(BF)
        for e, ic in enumerate(cores):
            gg[izh, iy, ic, 0:256] = gdn[256 * e : 256 * e + 256, 0:128]
            gg[izh, iy, ic, 256:512] = gdn[256 * e : 256 * e + 256, 128:256]
        gn[...] += mm(gh, up, 1, 1)
        gup = mm(nlt[...], gh)
        for e, r in enumerate(at):
            both = [gup[:, 256 * e + h : 256 * e + h + 128].reshape(NF, 8, 128) for h in (0, 128)]
            gg[:, :, :, r, :] = (
                jnp.concatenate(both, axis=1).astype(BF).reshape(NZH, NY, NC, 16, 128)
            )

    down = pl.ds(0, CUT)

    def core_copy(h, i):
        izh = (zh + h) % NZH
        return remote(
            gg.at[izh, i, 1 - c, down], rc.at[izh, i, down], co_s, co_r, h * NY + i, sibling
        )

    def hidden_loop(h, first, last):
        @pl.loop(first, last)
        def _(i):
            izh = (zh + h) % NZH
            hidden_units(izh, i)
            core_copy(h, i).start()

    r1a = []

    def down_sums(h):
        izh = (zh + h) % NZH
        for i in range(NY):
            core_copy(h, i).wait()
        for k in (1, 3, 2, 0):
            to = (y + k) % NY

            @pl.loop(0, CUT // 128)
            def _(i, to=to):
                r = rows(i * 128, 128)
                sa[to, izh, r] = (
                    gg[izh, to, c, r].astype(F32) + rc[izh, to, r].astype(F32)
                ).astype(BF)

            if k:
                r1a.append(reduce(sa.at[to, izh, down], rya.at[k - 1, izh], near_y[k]))

    hidden_loop(0, 0, 2)
    late = [to_sibling(1, i) for i in range(nx // 2)]
    hidden_loop(0, 2, NY)
    late += [to_sibling(1, i) for i in range(nx // 2, nx)]
    down_sums(0)
    for s in late:
        s.wait_recv()
    hidden_loop(1, 0, NY)
    upper = pl.ds(CUT, MAIN - CUT)
    r0 = reduce(gg.at[:, :, 1 - c, upper], rc.at[:, :, upper], sibling)
    down_sums(1)
    r0.wait_recv()
    r1b = []
    for k in [*range(1, nx), 0]:
        at = rows(CUT + ((x + k) % nx) * xb, xb)

        @pl.loop(0, NY)
        def _(i, at=at):
            sa[i, :, at] = (gg[:, i, c, at].astype(F32) + rc[:, i, at].astype(F32)).astype(BF)

        if k:
            r1b.append(reduce(sa.at[:, :, at], rxb.at[k - 1], near_x[k]))

    gnorm = gn[...]
    gfm = inv * (
        gnorm
        - jnp.mean(gnorm, axis=-1, keepdims=True)
        - normed * jnp.mean(gnorm * normed, axis=-1, keepdims=True)
    )
    gfm = gfm.astype(BF)
    gcomp = mm(emb, gfm, 0, 0).astype(BF)
    gproj = mm(emb, gcomp).astype(BF)
    gg[:, :, :, MAIN:ROWS, :] = gproj.reshape(NZH, NY, NC, 16, 128)
    r0 = reduce(gg.at[:, :, 1 - c, tail], rc.at[:, :, tail], sibling)
    gemb = (mm(gfm, compressed, 1, 1) + mm(proj, gcomp, 1, 1)).astype(BF)

    row = lax.broadcasted_iota(jnp.int32, (feats, feats), 0)
    col = lax.broadcasted_iota(jnp.int32, (feats, feats), 1)
    across_f = jnp.broadcast_to(own_ref[...].astype(F32), (feats, feats))
    down_f = jnp.sum(jnp.where(row == col, across_f, 0.0), axis=1, keepdims=True)
    within = jnp.sum(
        jnp.where((across_f == down_f) & (row < col), 1.0, 0.0), axis=0, keepdims=True
    )
    owner = across_f[0:1]
    owner_x = jnp.floor(owner * (1.0 / nzl))
    place = (owner - owner_x * nzl) * zrows + owner_x * per + within
    perm = jnp.where(row.astype(F32) == place, 1.0, 0.0).astype(BF)
    av1[...] = mm(perm, gemb).astype(BF)
    if nm > 5:
        pl.semaphore_wait(met.at[1], nq - 1)
    a1 = []
    mine = rows(zl * zrows, zrows)
    for k in range(1, nzl):
        to = (zl + k) % nzl
        a1.append(exchange(av1.at[rows(to * zrows, zrows)], av2.at[mine], dev(zl=to)))
    av2[mine] = av1[mine]

    r0.wait_recv()
    r1t = []
    for k in (1, 3, 2, 0):
        to = (y + k) % NY
        sa[to, :, tail] = (gg[:, to, c, tail].astype(F32) + rc[:, to, tail].astype(F32)).astype(BF)
        if k:
            r1t.append(reduce(sa.at[to, :, tail], ryt.at[k - 1], near_y[k]))

    for s in r1a:
        s.wait_recv()
    r2 = []
    for k in [*range(1, nx), 0]:
        at = rows(((x + k) % nx) * xa, xa)
        t = sa[y, :, at].astype(F32)
        for j in range(NY - 1):
            t += rya[j, :, at].astype(F32)
        sba[:, at] = t.astype(BF)
        if k:
            r2.append(reduce(sba.at[:, at], rxa.at[k - 1], near_x[k]))
    for s in r1b:
        s.wait_recv()
    at = rows(CUT + x * xb, xb)
    for k in (1, 3, 2, 0):
        to = (y + k) % NY
        t = sa[to, :, at].astype(F32)
        for j in range(nx - 1):
            t += rxb[j, to].astype(F32)
        sbb[to] = t.astype(BF)
        if k:
            r2.append(reduce(sbb.at[to], ryb.at[k - 1], near_y[k]))
    for s in r1t:
        s.wait_recv()
    t = sa[y, :, tail].astype(F32)
    for j in range(NY - 1):
        t += ryt[j].astype(F32)
    st[...] = t.astype(BF)
    r2 += [reduce(st, rxt.at[k - 1], near_x[k]) for k in range(1, nx)]
    for s in r2:
        s.wait_recv()
    ta = sba[:, rows(x * xa, xa)].astype(F32)
    for j in range(nx - 1):
        ta += rxa[j].astype(F32)
    tb = sbb[y].astype(F32)
    for j in range(NY - 1):
        tb += ryb[j].astype(F32)
    tt = st[...].astype(F32)
    for j in range(nx - 1):
        tt += rxt[j].astype(F32)
    t = jnp.concatenate([ta, tb], axis=1)
    for j in range(nq):
        sc[:, j] = jnp.concatenate([t[:, j * pq : (j + 1) * pq], tt], axis=1).astype(BF)

    r3 = []
    for k in range(1, nq):
        to = (q + k) % nq
        r3.append(reduce(sc.at[:, to], rq.at[k - 1], dev(zl=b * nq + to)))
    for s in r3:
        s.wait_recv()
    t = sc[:, q].astype(F32)
    for j in range(nq - 1):
        t += rq[j].astype(F32)
    se[...] = t.astype(BF)

    r4 = []
    for k in range(NZH * nb - 1, 0, -1):
        h2, b2 = (zh + k // nb) % NZH, (b + k % nb) % nb
        r4.append(reduce(se.at[h2], rb.at[k - 1], dev(zh=h2, zl=b2 * nq + q)))

    for s in a1:
        s.wait_recv()
    r_z, r_x, r_k = col // zrows, (col % zrows) // per, col % per
    perm = jnp.where(row == r_x * (nzl * per) + r_z * per + r_k, 1.0, 0.0).astype(BF)
    av3[...] = mm(perm, av2[...]).astype(BF)
    a2 = []
    xrows = nzl * per
    mine = rows(x * xrows, xrows)
    for k in range(1, nx):
        to = (x + k) % nx
        a2.append(exchange(av3.at[rows(to * xrows, xrows)], av4.at[mine], near_x[k]))
    av4[mine] = av3[mine]

    for s in r4:
        s.wait_recv()
    t = se[zh].astype(F32)
    for j in range(NZH * nb - 1):
        t += rb[j].astype(F32)
    t_proj = t[pq:qp]
    ox[x, q] = t[0:pq].astype(BF)

    step = [reduce(ox.at[x, q], ox.at[x, q], dev(zl=b * nq + (q + k) % nq)) for k in range(1, nq)]
    last = [reduce(ox.at[x, q], ox.at[x, q], to) for to in near_x.values()]
    for k, copy in enumerate(step, 1):
        copy.wait_recv()
        ref = ox.at[x, (q - k + nq) % nq]
        last += [reduce(ref, ref, to) for to in near_x.values()]
    for s in a2:
        s.wait_recv()
    owned_ref[...] = av4[...]
    for s in last:
        s.wait_recv()

    scale = 1.0 / (nx * nzl * NF)

    def unit(i):
        at = i * 16
        px, at = (at // xa, at % xa) if at < CUT else ((at - CUT) // xb, xa + (at - CUT) % xb)
        return ox[px, at // pq, at % pq : at % pq + 16, :].astype(F32) * scale

    for i in range(16):
        gdn_ref[16 * i : 16 * i + 16, 0:128] = unit(i)
        gdn_ref[16 * i : 16 * i + 16, 128:256] = unit(16 + i)
        t = unit(32 + i)
        gup_ref[:, 256 * i : 256 * i + 128] = t[0:8]
        gup_ref[:, 256 * i + 128 : 256 * i + 256] = t[8:16]
    gproj_ref[...] = t_proj * scale
    for s in pending:
        s.wait_send()


def per_device(split, embeddings, cotangent, owners, projection, up_weight, down_weight):
    nx, nzl, nq = split
    nb = nzl // nq
    feats, width = embeddings.shape[1:]
    xa = CUT // nx
    xb = (MAIN - CUT) // nx
    pq = (xa + xb) // nq
    qp = pq + ROWS - MAIN
    n_ag = 21 + 2 * (nx * NY - 1) + 3 + 2 * nx
    n_rs = 2 + 4 * (NY - 1) + 3 * (nx - 1) + 2 * (nq - 1) + (NZH * nb - 1) + nq * (nx - 1) + 3
    n_aa = nzl - 1 + nx - 1
    vmem = pl.BlockSpec(memory_space=pltpu.VMEM)
    return pl.pallas_call(
        functools.partial(kernel, split),
        out_shape=(
            jax.ShapeDtypeStruct((feats, width), BF),
            jax.ShapeDtypeStruct(projection.shape, F32),
            jax.ShapeDtypeStruct(up_weight.shape, F32),
            jax.ShapeDtypeStruct(down_weight.shape, F32),
        ),
        in_specs=[pl.BlockSpec(memory_space=pl.ANY)] * 6,
        out_specs=(vmem,) * 4,
        scratch_shapes=[
            pltpu.VMEM((feats, width), BF),
            pltpu.VMEM((feats, width), BF),
            pltpu.VMEM(owners.shape, jnp.int32),
            pltpu.VMEM(up_weight.shape, BF),
            pltpu.VMEM((NZH, NY, NC, ROWS, 128), BF),
            pltpu.VMEM((NZH, NY, NC, ROWS, 128), BF),
            pltpu.VMEM((NZH, NY, ROWS, 128), BF),
            pltpu.VMEM((NY, NZH, ROWS, 128), BF),
            pltpu.VMEM((NY - 1, NZH, CUT, 128), BF),
            pltpu.VMEM((NZH, CUT, 128), BF),
            pltpu.VMEM((nx - 1, NZH, xa, 128), BF),
            pltpu.VMEM((nx - 1, NY, NZH, xb, 128), BF),
            pltpu.VMEM((NY, NZH, xb, 128), BF),
            pltpu.VMEM((NY - 1, NZH, xb, 128), BF),
            pltpu.VMEM((NY - 1, NZH, ROWS - MAIN, 128), BF),
            pltpu.VMEM((NZH, ROWS - MAIN, 128), BF),
            pltpu.VMEM((nx - 1, NZH, ROWS - MAIN, 128), BF),
            pltpu.VMEM((NZH, nq, qp, 128), BF),
            pltpu.VMEM((nq - 1, NZH, qp, 128), BF),
            pltpu.VMEM((NZH, qp, 128), BF),
            pltpu.VMEM((NZH * nb - 1, qp, 128), BF),
            pltpu.VMEM((nx, nq, pq, 128), BF),
            pltpu.VMEM((feats, 128), BF),
            pltpu.VMEM((128, feats), BF),
            pltpu.VMEM((feats, 128), F32),
            pltpu.VMEM((feats, width), BF),
            pltpu.VMEM((feats, width), BF),
            pltpu.VMEM((feats, width), BF),
            pltpu.VMEM((feats, width), BF),
            pltpu.SemaphoreType.DMA((7,)),
            pltpu.SemaphoreType.DMA((n_ag,)),
            pltpu.SemaphoreType.DMA((n_ag,)),
            pltpu.SemaphoreType.DMA((NZH * NY,)),
            pltpu.SemaphoreType.DMA((NZH * NY,)),
            pltpu.SemaphoreType.DMA((n_rs,)),
            pltpu.SemaphoreType.DMA((n_rs,)),
            pltpu.SemaphoreType.DMA((n_aa,)),
            pltpu.SemaphoreType.DMA((n_aa,)),
            pltpu.SemaphoreType.REGULAR((2,)),
        ],
        compiler_params=pltpu.CompilerParams(
            collective_id=0, has_side_effects=True, vmem_limit_bytes=56 * 1024 * 1024
        ),
        name="layer_backward",
    )(embeddings, cotangent, owners, projection, up_weight, down_weight)


def solution(mesh):
    return jax.shard_map(
        functools.partial(per_device, SPLITS[mesh.shape["dp"]]),
        mesh=mesh,
        in_specs=(
            P(("dp", "fsdp"), None, None),
            P(("dp", "fsdp"), None, None),
            P(("dp", "fsdp"), None),
            P("fsdp", None),
            P("fsdp", None),
            P("fsdp", None),
        ),
        out_specs=(P(("dp", "fsdp"), None), P("fsdp", None), P("fsdp", None), P("fsdp", None)),
        check_vma=False,
    )
```

```python
import functools

import jax
import jax.numpy as jnp
from jax import lax
from jax.experimental import pallas as pl
from jax.experimental.pallas import tpu as pltpu
from jax.sharding import PartitionSpec as P

BF = jnp.bfloat16
F32 = jnp.float32
SPLITS = {64: (4, 16, 4), 4: (2, 2, 2), 8: (2, 4, 2)}
NZH, NY, NC = 2, 4, 2
NF = NZH * NY * NC
MAIN, ROWS = 768, 784
CUT, DOWN = 384, 512
HALF = (MAIN - DOWN) // 2


def mm(a, b, ca=1, cb=0):
    return lax.dot_general(a, b, (((ca,), (cb,)), ((), ())), preferred_element_type=F32)


def kernel(
    split, x_hbm, cot_hbm, own_hbm, proj_hbm, up_hbm, dn_hbm,
    owned_ref, gproj_ref, gup_ref, gdn_ref,
    x_ref, cot_ref, own_ref, up_ref,
    wg, gg, rc, sa, rya, sba, rxa, rxb, sbb, ryb, ryt, st, rxt, sc, rq, se, rb, ox,
    nl, nlt, gn, av1, av2, av3, av4,
    in_s, ag_s, ag_r, co_s, co_r, rs_s, rs_r, aa_s, aa_r, met,
):
    nx, nzl, nq = split
    nb = nzl // nq
    feats = x_ref.shape[0]
    xa, xb = rxa.shape[2], rxb.shape[3]
    xp, qp = xa + xb, se.shape[1]
    pq = xp // nq
    zrows = feats // nzl
    per = zrows // nx
    dp, fs = lax.axis_index("dp"), lax.axis_index("fsdp")
    x, zl = dp // nzl, dp % nzl
    zh, y, c = fs // (NY * NC), (fs // NC) % NY, fs % NC
    q, b = zl % nq, zl // nq

    def dev(x=x, zl=zl, zh=zh, y=y, c=c):
        return {"dp": x * nzl + zl, "fsdp": (zh * NY + y) * NC + c}

    pending = []

    def remote(src, dst, ssem, rsem, i, to):
        return pltpu.make_async_remote_copy(
            src_ref=src, dst_ref=dst, send_sem=ssem.at[i], recv_sem=rsem.at[i],
            device_id=to, device_id_type=pl.DeviceIdType.MESH,
        )

    def sender(ssem, rsem):
        count = [0]

        def send(src, dst, to):
            copy = remote(src, dst, ssem, rsem, count[0], to)
            count[0] += 1
            copy.start()
            pending.append(copy)
            return copy

        return send

    def rows(start, size):
        return pl.ds(pl.multiple_of(start, 16), size)

    gather, reduce, exchange = sender(ag_s, ag_r), sender(rs_s, rs_r), sender(aa_s, aa_r)
    sibling = dev(c=1 - c)
    near_y = {k: dev(y=(y + k) % NY) for k in (1, 3, 2)}
    near_x = {k: dev(x=(x + k) % nx) for k in range(1, nx)}

    barrier = pltpu.get_barrier_semaphore()
    peers = [sibling]
    peers += [
        dev(x=(x + i) % nx, y=(y + k) % NY) for i in range(nx) for k in range(NY) if i or k
    ]
    peers += [dev(zl=b * nq + (q + k) % nq) for k in range(1, nq)]
    m, nm = zh * nb + b, NZH * nb

    def ring(k):
        to = (m + k) % nm
        return dev(zh=to // nb, zl=(to % nb) * nq + q)

    peers += [ring(k) for k in range(1, nm) if min(k, nm - k) <= 2]
    half = (zl + nzl // 2) % nzl
    if (nzl // 2) % nq:
        peers.append(dev(zh=1 - zh, zl=half))

    def tell(i, to):
        pl.semaphore_signal(met.at[i], inc=1, device_id=to, device_id_type=pl.DeviceIdType.MESH)

    for p in peers:
        pl.semaphore_signal(barrier, inc=1, device_id=p, device_id_type=pl.DeviceIdType.MESH)

    inputs = [
        pltpu.make_async_copy(src, dst, in_s.at[i])
        for i, (src, dst) in enumerate(
            (
                (up_hbm, up_ref),
                (proj_hbm, wg.at[zh, y, c, MAIN:ROWS]),
                (dn_hbm.at[:, 0:128], wg.at[zh, y, c, 0:256]),
                (dn_hbm.at[:, 128:256], wg.at[zh, y, c, 256:512]),
                (x_hbm.at[0], x_ref),
                (own_hbm, own_ref),
                (cot_hbm.at[0], cot_ref),
            )
        )
    ]
    for copy in inputs:
        copy.start()
    inputs[0].wait()
    for u in range(NF):
        lo = up_ref[:, 256 * u : 256 * u + 128].astype(F32)
        hi = up_ref[:, 256 * u + 128 : 256 * u + 256].astype(F32)
        wg[zh, y, c, 512 + 16 * u : 528 + 16 * u] = jnp.concatenate([lo, hi], axis=0).astype(BF)
    for copy in inputs[1:4]:
        copy.wait()
    pl.semaphore_wait(barrier, len(peers))
    if nm > 5:
        tell(0, ring(2))
        tell(0, ring(nm - 2))

    parts = ((DOWN, (MAIN - DOWN) // nx), (0, DOWN // nx))
    main, tail = pl.ds(0, MAIN), pl.ds(MAIN, ROWS - MAIN)
    oz = 1 - zh
    own, other = wg.at[zh, y, c], wg.at[oz, y, c]
    far = dev(zh=oz, zl=half)

    def swap(ref, to):
        return gather(ref, ref, to)

    far_main = []
    for base, size in parts:
        far_main.append(swap(own.at[rows(base + x * size, size)], far))
        if base:
            far_tail = swap(own.at[tail], far)
    tails = [swap(own.at[tail], to) for to in near_y.values()]
    to_core = [swap(own.at[tail], sibling)]
    mains = [swap(own.at[main], to) for to in near_y.values()]
    mains_core = [swap(own.at[main], sibling)]
    for k, copy in zip(near_y, tails):
        copy.wait_recv()
        to_core.append(swap(wg.at[zh, (y - k + NY) % NY, c, tail], sibling))
    shares = {}
    for n, (base, size) in enumerate(parts):
        far_main[n].wait_recv()
        piece = rows(base + x * size, size)
        for i in range(nx):
            for k in (1, 3, 2, 0):
                if i or k:
                    shares[n, i, k] = swap(
                        other.at[piece], dev(x=(x + i) % nx, y=(y + k) % NY)
                    )
        if n == 0:
            far_tail.wait_recv()
            tails = [swap(other.at[tail], to) for to in near_y.values()]
            to_core.append(swap(other.at[tail], sibling))
    for k, copy in zip(near_y, tails):
        copy.wait_recv()
        to_core.append(swap(wg.at[oz, (y - k + NY) % NY, c, tail], sibling))
    for k, copy in zip(near_y, mains):
        copy.wait_recv()
        mains_core.append(swap(wg.at[zh, (y - k + NY) % NY, c, main], sibling))

    if nm > 5:
        pl.semaphore_wait(met.at[0], 2)
        for k in range(1, nq):
            tell(1, dev(zl=b * nq + (q + k) % nq))

    def to_sibling(n, i):
        base, size = parts[n]
        for k in range(NY):
            if i or k:
                shares[n, i, k].wait_recv()
        at = rows(base + ((x - i + nx) % nx) * size, size)
        return swap(wg.at[oz, :, c, at], sibling)

    for s in to_core:
        s.wait_recv()
    inputs[4].wait()
    emb = x_ref[...]
    proj = wg[:, :, :, MAIN:ROWS, :].reshape(feats, 128)
    compressed = mm(emb, proj, 0, 0).astype(BF)
    fm = mm(emb, compressed)
    centre = fm - jnp.mean(fm, axis=-1, keepdims=True)
    inv = lax.rsqrt(jnp.mean(centre * centre, axis=-1, keepdims=True) + 1e-05)
    normed = centre * inv
    nl[...] = normed.astype(BF)
    nlt[...] = normed.T.astype(BF)
    gn[...] = jnp.zeros_like(gn)
    inputs[5].wait()
    inputs[6].wait()

    mains_core += [to_sibling(0, i) for i in range(nx)]
    for s in mains_core:
        s.wait_recv()

    def hidden_units(izh, iy):
        cores = (1 - c, c)
        at = [rows(512 + 16 * ((izh * NY + iy) * NC + ic), 16) for ic in cores]
        pieces = [wg[:, :, :, r, :].reshape(NF, 16, 128).astype(F32) for r in at]
        up = jnp.concatenate(
            [p[:, e : e + 8].reshape(128, 128) for p in pieces for e in (0, 8)], axis=1
        ).astype(BF)
        downs = jnp.concatenate(
            [
                jnp.concatenate([wg[izh, iy, ic, 0:256], wg[izh, iy, ic, 256:512]], axis=1)
                for ic in cores
            ],
            axis=0,
        )
        cots = cot_ref[...]
        hidden = mm(nl[...], up)
        sig = 0.5 * jnp.tanh(0.5 * hidden) + 0.5
        act = (hidden * sig).astype(BF)
        gh = (mm(cots, downs, 1, 1) * sig * (1.0 + hidden * (1.0 - sig))).astype(BF)
        gdn = mm(act, cots, 0, 0).astype(BF)
        for e, ic in enumerate(cores):
            gg[izh, iy, ic, 0:256] = gdn[256 * e : 256 * e + 256, 0:128]
            gg[izh, iy, ic, 256:512] = gdn[256 * e : 256 * e + 256, 128:256]
        gn[...] += mm(gh, up, 1, 1)
        gup = mm(nlt[...], gh)
        for e, r in enumerate(at):
            both = [gup[:, 256 * e + h : 256 * e + h + 128].reshape(NF, 8, 128) for h in (0, 128)]
            gg[:, :, :, r, :] = (
                jnp.concatenate(both, axis=1).astype(BF).reshape(NZH, NY, NC, 16, 128)
            )

    down, first = pl.ds(0, DOWN), pl.ds(0, CUT)
    xd, xu = (DOWN - CUT) // nx, HALF // nx

    def core_copy(h, i):
        izh = (zh + h) % NZH
        return remote(
            gg.at[izh, i, 1 - c, down], rc.at[izh, i, down], co_s, co_r, h * NY + i, sibling
        )

    def hidden_loop(h):
        @pl.loop(0, NY)
        def _(i):
            izh = (zh + h) % NZH
            hidden_units(izh, i)
            core_copy(h, i).start()

    def add(at):
        sa_at, gg_at, rc_at = at
        sa[sa_at] = (gg[gg_at].astype(F32) + rc[rc_at].astype(F32)).astype(BF)

    r1a, r1b = [], []

    def upper(h):
        at = rows(DOWN + HALF * ((zh + h) % NZH), HALF)
        return reduce(gg.at[:, :, 1 - c, at], rc.at[:, :, at], sibling)

    def first_sums(h, r0):
        izh = (zh + h) % NZH
        for i in range(NY):
            core_copy(h, i).wait()
        for k in (1, 3, 2, 0):
            to = (y + k) % NY

            @pl.loop(0, CUT // 128)
            def _(i, to=to):
                r = rows(i * 128, 128)
                add(((to, izh, r), (izh, to, c, r), (izh, to, r)))

            if k:
                r1a.append(reduce(sa.at[to, izh, first], rya.at[k - 1, izh], near_y[k]))
        r0.wait_recv()
        for k in [*range(1, nx), 0]:
            to = (x + k) % nx
            lo, hi = rows(CUT + to * xd, xd), rows(DOWN + HALF * izh + to * xu, xu)

            @pl.loop(0, NY)
            def _(i, lo=lo, hi=hi):
                add(((i, izh, lo), (izh, i, c, lo), (izh, i, lo)))
                for z in range(NZH):
                    add(((i, z, hi), (z, i, c, hi), (z, i, hi)))

            if k:
                land = rxb.at[k - 1, :, izh, 0:xd]
                r1b.append(reduce(sa.at[:, izh, lo], land, near_x[k]))
                land = rxb.at[k - 1, :, :, rows(xd + xu * izh, xu)]
                r1b.append(reduce(sa.at[:, :, hi], land, near_x[k]))

    hidden_loop(0)
    r0 = upper(0)
    first_sums(0, r0)
    late = [to_sibling(1, i) for i in range(nx)]
    for s in late:
        s.wait_recv()
    hidden_loop(1)
    r0 = upper(1)
    first_sums(1, r0)

    gnorm = gn[...]
    gfm = inv * (
        gnorm
        - jnp.mean(gnorm, axis=-1, keepdims=True)
        - normed * jnp.mean(gnorm * normed, axis=-1, keepdims=True)
    )
    gfm = gfm.astype(BF)
    gcomp = mm(emb, gfm, 0, 0).astype(BF)
    gproj = mm(emb, gcomp).astype(BF)
    gg[:, :, :, MAIN:ROWS, :] = gproj.reshape(NZH, NY, NC, 16, 128)
    r0 = reduce(gg.at[:, :, 1 - c, tail], rc.at[:, :, tail], sibling)
    gemb = (mm(gfm, compressed, 1, 1) + mm(proj, gcomp, 1, 1)).astype(BF)

    row = lax.broadcasted_iota(jnp.int32, (feats, feats), 0)
    col = lax.broadcasted_iota(jnp.int32, (feats, feats), 1)
    across_f = jnp.broadcast_to(own_ref[...].astype(F32), (feats, feats))
    down_f = jnp.sum(jnp.where(row == col, across_f, 0.0), axis=1, keepdims=True)
    within = jnp.sum(
        jnp.where((across_f == down_f) & (row < col), 1.0, 0.0), axis=0, keepdims=True
    )
    owner = across_f[0:1]
    owner_x = jnp.floor(owner * (1.0 / nzl))
    place = (owner - owner_x * nzl) * zrows + owner_x * per + within
    perm = jnp.where(row.astype(F32) == place, 1.0, 0.0).astype(BF)
    av1[...] = mm(perm, gemb).astype(BF)
    if nm > 5:
        pl.semaphore_wait(met.at[1], nq - 1)
    a1 = []
    mine = rows(zl * zrows, zrows)
    for k in range(1, nzl):
        to = (zl + k) % nzl
        a1.append(exchange(av1.at[rows(to * zrows, zrows)], av2.at[mine], dev(zl=to)))
    av2[mine] = av1[mine]

    r0.wait_recv()
    r1t = []
    for k in (1, 3, 2, 0):
        to = (y + k) % NY
        sa[to, :, tail] = (gg[:, to, c, tail].astype(F32) + rc[:, to, tail].astype(F32)).astype(BF)
        if k:
            r1t.append(reduce(sa.at[to, :, tail], ryt.at[k - 1], near_y[k]))

    for s in r1a:
        s.wait_recv()
    r2 = []
    for k in [*range(1, nx), 0]:
        at = rows(((x + k) % nx) * xa, xa)
        t = sa[y, :, at].astype(F32)
        for j in range(NY - 1):
            t += rya[j, :, at].astype(F32)
        sba[:, at] = t.astype(BF)
        if k:
            r2.append(reduce(sba.at[:, at], rxa.at[k - 1], near_x[k]))
    for s in r1b:
        s.wait_recv()
    mine = (rows(CUT + x * xd, xd), rows(DOWN + x * xu, xu), rows(DOWN + HALF + x * xu, xu))
    for k in (1, 3, 2, 0):
        to = (y + k) % NY
        t = jnp.concatenate([sa[to, :, at] for at in mine], axis=1).astype(F32)
        for j in range(nx - 1):
            t += rxb[j, to].astype(F32)
        sbb[to] = t.astype(BF)
        if k:
            r2.append(reduce(sbb.at[to], ryb.at[k - 1], near_y[k]))
    for s in r1t:
        s.wait_recv()
    t = sa[y, :, tail].astype(F32)
    for j in range(NY - 1):
        t += ryt[j].astype(F32)
    st[...] = t.astype(BF)
    r2 += [reduce(st, rxt.at[k - 1], near_x[k]) for k in range(1, nx)]
    for s in r2:
        s.wait_recv()
    ta = sba[:, rows(x * xa, xa)].astype(F32)
    for j in range(nx - 1):
        ta += rxa[j].astype(F32)
    tb = sbb[y].astype(F32)
    for j in range(NY - 1):
        tb += ryb[j].astype(F32)
    tt = st[...].astype(F32)
    for j in range(nx - 1):
        tt += rxt[j].astype(F32)
    t = jnp.concatenate([ta, tb], axis=1)
    for j in range(nq):
        sc[:, j] = jnp.concatenate([t[:, j * pq : (j + 1) * pq], tt], axis=1).astype(BF)

    r3 = []
    for k in range(1, nq):
        to = (q + k) % nq
        r3.append(reduce(sc.at[:, to], rq.at[k - 1], dev(zl=b * nq + to)))
    for s in r3:
        s.wait_recv()
    t = sc[:, q].astype(F32)
    for j in range(nq - 1):
        t += rq[j].astype(F32)
    se[...] = t.astype(BF)

    r4 = []
    for k in range(NZH * nb - 1, 0, -1):
        h2, b2 = (zh + k // nb) % NZH, (b + k % nb) % nb
        r4.append(reduce(se.at[h2], rb.at[k - 1], dev(zh=h2, zl=b2 * nq + q)))

    for s in a1:
        s.wait_recv()
    r_z, r_x, r_k = col // zrows, (col % zrows) // per, col % per
    perm = jnp.where(row == r_x * (nzl * per) + r_z * per + r_k, 1.0, 0.0).astype(BF)
    av3[...] = mm(perm, av2[...]).astype(BF)
    a2 = []
    xrows = nzl * per
    mine = rows(x * xrows, xrows)
    for k in range(1, nx):
        to = (x + k) % nx
        a2.append(exchange(av3.at[rows(to * xrows, xrows)], av4.at[mine], near_x[k]))
    av4[mine] = av3[mine]

    for s in r4:
        s.wait_recv()
    t = se[zh].astype(F32)
    for j in range(NZH * nb - 1):
        t += rb[j].astype(F32)
    t_proj = t[pq:qp]
    ox[x, q] = t[0:pq].astype(BF)

    step = [reduce(ox.at[x, q], ox.at[x, q], dev(zl=b * nq + (q + k) % nq)) for k in range(1, nq)]
    last = [reduce(ox.at[x, q], ox.at[x, q], to) for to in near_x.values()]
    for k, copy in enumerate(step, 1):
        copy.wait_recv()
        ref = ox.at[x, (q - k + nq) % nq]
        last += [reduce(ref, ref, to) for to in near_x.values()]
    for s in a2:
        s.wait_recv()
    owned_ref[...] = av4[...]
    for s in last:
        s.wait_recv()

    scale = 1.0 / (nx * nzl * NF)

    def unit(i):
        at = i * 16
        for base, size, off in (
            (0, xa, 0), (CUT, xd, xa), (DOWN, xu, xa + xd), (DOWN + HALF, xu, xa + xd + xu)
        ):
            if base <= i * 16 < base + size * nx:
                px, at = (i * 16 - base) // size, off + (i * 16 - base) % size
        return ox[px, at // pq, at % pq : at % pq + 16, :].astype(F32) * scale

    for i in range(16):
        gdn_ref[16 * i : 16 * i + 16, 0:128] = unit(i)
        gdn_ref[16 * i : 16 * i + 16, 128:256] = unit(16 + i)
        t = unit(32 + i)
        gup_ref[:, 256 * i : 256 * i + 128] = t[0:8]
        gup_ref[:, 256 * i + 128 : 256 * i + 256] = t[8:16]
    gproj_ref[...] = t_proj * scale
    for s in pending:
        s.wait_send()


def per_device(split, embeddings, cotangent, owners, projection, up_weight, down_weight):
    nx, nzl, nq = split
    nb = nzl // nq
    feats, width = embeddings.shape[1:]
    xa = CUT // nx
    xb = (MAIN - CUT) // nx
    pq = (xa + xb) // nq
    qp = pq + ROWS - MAIN
    n_ag = 21 + 2 * (nx * NY - 1) + 3 + 2 * nx
    n_rs = 3 + 4 * (NY - 1) + 6 * (nx - 1) + 2 * (nq - 1) + (NZH * nb - 1) + nq * (nx - 1) + 3
    n_aa = nzl - 1 + nx - 1
    vmem = pl.BlockSpec(memory_space=pltpu.VMEM)
    operands = [
        pltpu.with_memory_space_constraint(a, pltpu.HBM)
        for a in (embeddings, cotangent, owners, projection, up_weight, down_weight)
    ]
    return pl.pallas_call(
        functools.partial(kernel, split),
        out_shape=(
            jax.ShapeDtypeStruct((feats, width), BF),
            jax.ShapeDtypeStruct(projection.shape, F32),
            jax.ShapeDtypeStruct(up_weight.shape, F32),
            jax.ShapeDtypeStruct(down_weight.shape, F32),
        ),
        in_specs=[pl.BlockSpec(memory_space=pl.ANY)] * 6,
        out_specs=(vmem,) * 4,
        scratch_shapes=[
            pltpu.VMEM((feats, width), BF),
            pltpu.VMEM((feats, width), BF),
            pltpu.VMEM(owners.shape, jnp.int32),
            pltpu.VMEM(up_weight.shape, BF),
            pltpu.VMEM((NZH, NY, NC, ROWS, 128), BF),
            pltpu.VMEM((NZH, NY, NC, ROWS, 128), BF),
            pltpu.VMEM((NZH, NY, ROWS, 128), BF),
            pltpu.VMEM((NY, NZH, ROWS, 128), BF),
            pltpu.VMEM((NY - 1, NZH, CUT, 128), BF),
            pltpu.VMEM((NZH, CUT, 128), BF),
            pltpu.VMEM((nx - 1, NZH, xa, 128), BF),
            pltpu.VMEM((nx - 1, NY, NZH, xb, 128), BF),
            pltpu.VMEM((NY, NZH, xb, 128), BF),
            pltpu.VMEM((NY - 1, NZH, xb, 128), BF),
            pltpu.VMEM((NY - 1, NZH, ROWS - MAIN, 128), BF),
            pltpu.VMEM((NZH, ROWS - MAIN, 128), BF),
            pltpu.VMEM((nx - 1, NZH, ROWS - MAIN, 128), BF),
            pltpu.VMEM((NZH, nq, qp, 128), BF),
            pltpu.VMEM((nq - 1, NZH, qp, 128), BF),
            pltpu.VMEM((NZH, qp, 128), BF),
            pltpu.VMEM((NZH * nb - 1, qp, 128), BF),
            pltpu.VMEM((nx, nq, pq, 128), BF),
            pltpu.VMEM((feats, 128), BF),
            pltpu.VMEM((128, feats), BF),
            pltpu.VMEM((feats, 128), F32),
            pltpu.VMEM((feats, width), BF),
            pltpu.VMEM((feats, width), BF),
            pltpu.VMEM((feats, width), BF),
            pltpu.VMEM((feats, width), BF),
            pltpu.SemaphoreType.DMA((7,)),
            pltpu.SemaphoreType.DMA((n_ag,)),
            pltpu.SemaphoreType.DMA((n_ag,)),
            pltpu.SemaphoreType.DMA((NZH * NY,)),
            pltpu.SemaphoreType.DMA((NZH * NY,)),
            pltpu.SemaphoreType.DMA((n_rs,)),
            pltpu.SemaphoreType.DMA((n_rs,)),
            pltpu.SemaphoreType.DMA((n_aa,)),
            pltpu.SemaphoreType.DMA((n_aa,)),
            pltpu.SemaphoreType.REGULAR((2,)),
        ],
        compiler_params=pltpu.CompilerParams(
            collective_id=0, has_side_effects=True, vmem_limit_bytes=48 * 1024 * 1024
        ),
        name="layer_backward",
    )(*operands)


def solution(mesh):
    return jax.shard_map(
        functools.partial(per_device, SPLITS[mesh.shape["dp"]]),
        mesh=mesh,
        in_specs=(
            P(("dp", "fsdp"), None, None),
            P(("dp", "fsdp"), None, None),
            P(("dp", "fsdp"), None),
            P("fsdp", None),
            P("fsdp", None),
            P("fsdp", None),
        ),
        out_specs=(P(("dp", "fsdp"), None), P("fsdp", None), P("fsdp", None), P("fsdp", None)),
        check_vma=False,
    )
```

```python
import functools

import jax
import jax.numpy as jnp
from jax import lax
from jax.experimental import pallas as pl
from jax.experimental.pallas import tpu as pltpu
from jax.sharding import PartitionSpec as P

BF = jnp.bfloat16
F32 = jnp.float32
SPLITS = {64: (4, 16, 4), 4: (2, 2, 2), 8: (2, 4, 2)}
NZH, NY, NC = 2, 4, 2
NF = NZH * NY * NC
MAIN, ROWS = 768, 784
CUT, DOWN = 384, 512
HALF = (MAIN - DOWN) // 2


def mm(a, b, ca=1, cb=0):
    return lax.dot_general(a, b, (((ca,), (cb,)), ((), ())), preferred_element_type=F32)


def kernel(
    split, x_hbm, cot_hbm, own_hbm, proj_hbm, up_hbm, dn_hbm,
    owned_ref, gproj_ref, gup_ref, gdn_ref,
    x_ref, cot_ref, own_ref, up_ref,
    wg, gg, rc, sa, rya, sba, rxa, rxb, sbb, ryb, ryt, st, rxt, sc, rq, se, rb, ox,
    nl, nlt, gn, half_cot, to_z, to_x, av1, av2, av3, av4,
    in_s, ag_s, ag_r, co_s, co_r, rs_s, rs_r, aa_s, aa_r, met,
):
    nx, nzl, nq = split
    nb = nzl // nq
    feats = x_ref.shape[0]
    xa, xb = rxa.shape[2], rxb.shape[3]
    xp, qp = xa + xb, se.shape[1]
    pq = xp // nq
    zrows = feats // nzl
    per = zrows // nx
    dp, fs = lax.axis_index("dp"), lax.axis_index("fsdp")
    x, zl = dp // nzl, dp % nzl
    zh, y, c = fs // (NY * NC), (fs // NC) % NY, fs % NC
    q, b = zl % nq, zl // nq

    def dev(x=x, zl=zl, zh=zh, y=y, c=c):
        return {"dp": x * nzl + zl, "fsdp": (zh * NY + y) * NC + c}

    pending = []

    def remote(src, dst, ssem, rsem, i, to):
        return pltpu.make_async_remote_copy(
            src_ref=src, dst_ref=dst, send_sem=ssem.at[i], recv_sem=rsem.at[i],
            device_id=to, device_id_type=pl.DeviceIdType.MESH,
        )

    def sender(ssem, rsem):
        count = [0]

        def send(src, dst, to):
            copy = remote(src, dst, ssem, rsem, count[0], to)
            count[0] += 1
            copy.start()
            pending.append(copy)
            return copy

        return send

    def rows(start, size):
        return pl.ds(pl.multiple_of(start, 16), size)

    gather, reduce, exchange = sender(ag_s, ag_r), sender(rs_s, rs_r), sender(aa_s, aa_r)
    sibling = dev(c=1 - c)
    near_y = {k: dev(y=(y + k) % NY) for k in (1, 3, 2)}
    near_x = {k: dev(x=(x + k) % nx) for k in range(1, nx)}

    barrier = pltpu.get_barrier_semaphore()
    peers = [sibling]
    peers += [
        dev(x=(x + i) % nx, y=(y + k) % NY) for i in range(nx) for k in range(NY) if i or k
    ]
    peers += [dev(zl=b * nq + (q + k) % nq) for k in range(1, nq)]
    m, nm = zh * nb + b, NZH * nb

    def ring(k):
        to = (m + k) % nm
        return dev(zh=to // nb, zl=(to % nb) * nq + q)

    peers += [ring(k) for k in range(1, nm) if min(k, nm - k) <= 2]
    half = (zl + nzl // 2) % nzl
    if (nzl // 2) % nq:
        peers.append(dev(zh=1 - zh, zl=half))

    def tell(i, to):
        pl.semaphore_signal(met.at[i], inc=1, device_id=to, device_id_type=pl.DeviceIdType.MESH)

    for p in peers:
        pl.semaphore_signal(barrier, inc=1, device_id=p, device_id_type=pl.DeviceIdType.MESH)

    inputs = [
        pltpu.make_async_copy(src, dst, in_s.at[i])
        for i, (src, dst) in enumerate(
            (
                (up_hbm, up_ref),
                (proj_hbm, wg.at[zh, y, c, MAIN:ROWS]),
                (dn_hbm.at[:, 0:128], wg.at[zh, y, c, 0:256]),
                (dn_hbm.at[:, 128:256], wg.at[zh, y, c, 256:512]),
                (x_hbm.at[0], x_ref),
                (own_hbm, own_ref),
                (cot_hbm.at[0], cot_ref),
            )
        )
    ]
    for copy in inputs:
        copy.start()
    inputs[0].wait()
    for u in range(NF):
        lo = up_ref[:, 256 * u : 256 * u + 128].astype(F32)
        hi = up_ref[:, 256 * u + 128 : 256 * u + 256].astype(F32)
        wg[zh, y, c, 512 + 16 * u : 528 + 16 * u] = jnp.concatenate([lo, hi], axis=0).astype(BF)
    for copy in inputs[1:4]:
        copy.wait()
    pl.semaphore_wait(barrier, len(peers))
    if nm > 5:
        tell(0, ring(2))
        tell(0, ring(nm - 2))

    parts = ((DOWN, (MAIN - DOWN) // nx), (0, DOWN // nx))
    main, tail = pl.ds(0, MAIN), pl.ds(MAIN, ROWS - MAIN)
    oz = 1 - zh
    own, other = wg.at[zh, y, c], wg.at[oz, y, c]
    far = dev(zh=oz, zl=half)

    def swap(ref, to):
        return gather(ref, ref, to)

    far_main = []
    for base, size in parts:
        far_main.append(swap(own.at[rows(base + x * size, size)], far))
        if base:
            far_tail = swap(own.at[tail], far)
    tails = [swap(own.at[tail], to) for to in near_y.values()]
    to_core = [swap(own.at[tail], sibling)]
    mains = [swap(own.at[main], to) for to in near_y.values()]
    mains_core = [swap(own.at[main], sibling)]
    for k, copy in zip(near_y, tails):
        copy.wait_recv()
        to_core.append(swap(wg.at[zh, (y - k + NY) % NY, c, tail], sibling))
    shares = {}
    for n, (base, size) in enumerate(parts):
        far_main[n].wait_recv()
        piece = rows(base + x * size, size)
        for i in range(nx):
            for k in (1, 3, 2, 0):
                if i or k:
                    shares[n, i, k] = swap(
                        other.at[piece], dev(x=(x + i) % nx, y=(y + k) % NY)
                    )
        if n == 0:
            far_tail.wait_recv()
            tails = [swap(other.at[tail], to) for to in near_y.values()]
            to_core.append(swap(other.at[tail], sibling))
    for k, copy in zip(near_y, tails):
        copy.wait_recv()
        to_core.append(swap(wg.at[oz, (y - k + NY) % NY, c, tail], sibling))
    for k, copy in zip(near_y, mains):
        copy.wait_recv()
        mains_core.append(swap(wg.at[zh, (y - k + NY) % NY, c, main], sibling))

    if nm > 5:
        pl.semaphore_wait(met.at[0], 2)
        for k in range(1, nq):
            tell(1, dev(zl=b * nq + (q + k) % nq))

    def to_sibling(n, i):
        base, size = parts[n]
        for k in range(NY):
            if i or k:
                shares[n, i, k].wait_recv()
        at = rows(base + ((x - i + nx) % nx) * size, size)
        return swap(wg.at[oz, :, c, at], sibling)

    for s in to_core:
        s.wait_recv()
    inputs[4].wait()
    emb = x_ref[...]
    proj = wg[:, :, :, MAIN:ROWS, :].reshape(feats, 128)
    compressed = mm(emb, proj, 0, 0).astype(BF)
    fm = mm(emb, compressed)
    centre = fm - jnp.mean(fm, axis=-1, keepdims=True)
    inv = lax.rsqrt(jnp.mean(centre * centre, axis=-1, keepdims=True) + 1e-05)
    normed = centre * inv
    normed_t = normed.T
    nl[...] = (0.5 * normed_t).astype(BF)
    nlt[...] = normed_t.astype(BF)
    gn[...] = jnp.zeros_like(gn)
    inputs[5].wait()
    inputs[6].wait()
    half_cot[...] = (0.5 * cot_ref[...].astype(F32)).T.astype(BF)

    row = lax.broadcasted_iota(jnp.int32, (feats, feats), 0)
    col = lax.broadcasted_iota(jnp.int32, (feats, feats), 1)
    across_f = jnp.broadcast_to(own_ref[...].astype(F32), (feats, feats))
    down_f = jnp.sum(jnp.where(row == col, across_f, 0.0), axis=1, keepdims=True)
    within = jnp.sum(
        jnp.where((across_f == down_f) & (row < col), 1.0, 0.0), axis=0, keepdims=True
    )
    owner = across_f[0:1]
    owner_x = jnp.floor(owner * (1.0 / nzl))
    place = (owner - owner_x * nzl) * zrows + owner_x * per + within
    to_z[...] = jnp.where(row.astype(F32) == place, 1.0, 0.0).astype(BF)
    r_z, r_x, r_k = col // zrows, (col % zrows) // per, col % per
    to_x[...] = jnp.where(row == r_x * (nzl * per) + r_z * per + r_k, 1.0, 0.0).astype(BF)

    mains_core += [to_sibling(0, i) for i in range(nx)]
    for s in mains_core:
        s.wait_recv()

    def hidden_units(izh, iy):
        cores = (1 - c, c)
        at = [rows(512 + 16 * ((izh * NY + iy) * NC + ic), 16) for ic in cores]
        pieces = [wg[:, :, :, r, :].reshape(NF, 16, 128).astype(F32) for r in at]
        up = jnp.concatenate(
            [p[:, e : e + 8].reshape(128, 128) for p in pieces for e in (0, 8)], axis=1
        ).astype(BF)
        downs = jnp.concatenate(
            [
                jnp.concatenate([wg[izh, iy, ic, 0:256], wg[izh, iy, ic, 256:512]], axis=1)
                for ic in cores
            ],
            axis=0,
        )
        cots = cot_ref[...]
        half_hidden = mm(up, nl[...], 0, 0)
        t1 = jnp.tanh(half_hidden) + 1.0
        act32 = half_hidden * t1
        gh = (mm(downs, half_cot[...]) * (t1 + act32 * (2.0 - t1))).astype(BF)
        gdn = mm(act32.astype(BF), cots).astype(BF)
        for e, ic in enumerate(cores):
            gg[izh, iy, ic, 0:256] = gdn[256 * e : 256 * e + 256, 0:128]
            gg[izh, iy, ic, 256:512] = gdn[256 * e : 256 * e + 256, 128:256]
        gn[...] += mm(up, gh)
        gup = mm(nlt[...], gh, 1, 1)
        for e, r in enumerate(at):
            both = [gup[:, 256 * e + h : 256 * e + h + 128].reshape(NF, 8, 128) for h in (0, 128)]
            gg[:, :, :, r, :] = (
                jnp.concatenate(both, axis=1).astype(BF).reshape(NZH, NY, NC, 16, 128)
            )

    down, first = pl.ds(0, DOWN), pl.ds(0, CUT)
    xd, xu = (DOWN - CUT) // nx, HALF // nx

    def core_copy(h, i):
        izh = (zh + h) % NZH
        return remote(
            gg.at[izh, i, 1 - c, down], rc.at[izh, i, down], co_s, co_r, h * NY + i, sibling
        )

    def hidden_loop(h):
        @pl.loop(0, NY)
        def _(i):
            izh = (zh + h) % NZH
            hidden_units(izh, i)
            core_copy(h, i).start()

    def add(at):
        sa_at, gg_at, rc_at = at
        sa[sa_at] = (gg[gg_at].astype(F32) + rc[rc_at].astype(F32)).astype(BF)

    r1a, r1b = [], []

    def upper(h):
        at = rows(DOWN + HALF * ((zh + h) % NZH), HALF)
        return reduce(gg.at[:, :, 1 - c, at], rc.at[:, :, at], sibling)

    def first_sums(h, r0):
        izh = (zh + h) % NZH
        for i in range(NY):
            core_copy(h, i).wait()
        for k in (1, 3, 2, 0):
            to = (y + k) % NY

            @pl.loop(0, CUT // 128)
            def _(i, to=to):
                r = rows(i * 128, 128)
                add(((to, izh, r), (izh, to, c, r), (izh, to, r)))

            if k:
                r1a.append(reduce(sa.at[to, izh, first], rya.at[k - 1, izh], near_y[k]))
        r0.wait_recv()
        for k in [*range(1, nx), 0]:
            to = (x + k) % nx
            lo, hi = rows(CUT + to * xd, xd), rows(DOWN + HALF * izh + to * xu, xu)

            @pl.loop(0, NY)
            def _(i, lo=lo, hi=hi):
                add(((i, izh, lo), (izh, i, c, lo), (izh, i, lo)))
                for z in range(NZH):
                    add(((i, z, hi), (z, i, c, hi), (z, i, hi)))

            if k:
                land = rxb.at[k - 1, :, izh, 0:xd]
                r1b.append(reduce(sa.at[:, izh, lo], land, near_x[k]))
                land = rxb.at[k - 1, :, :, rows(xd + xu * izh, xu)]
                r1b.append(reduce(sa.at[:, :, hi], land, near_x[k]))

    hidden_loop(0)
    r0 = upper(0)
    first_sums(0, r0)
    late = [to_sibling(1, i) for i in range(nx)]
    for s in late:
        s.wait_recv()
    hidden_loop(1)
    r0 = upper(1)
    first_sums(1, r0)

    gnorm = gn[...].T
    gfm = inv * (
        gnorm
        - jnp.mean(gnorm, axis=-1, keepdims=True)
        - normed * jnp.mean(gnorm * normed, axis=-1, keepdims=True)
    )
    gfm = gfm.astype(BF)
    gcomp = mm(emb, gfm, 0, 0).astype(BF)
    gproj = mm(emb, gcomp).astype(BF)
    gg[:, :, :, MAIN:ROWS, :] = gproj.reshape(NZH, NY, NC, 16, 128)
    r0 = reduce(gg.at[:, :, 1 - c, tail], rc.at[:, :, tail], sibling)
    gemb = (mm(gfm, compressed, 1, 1) + mm(proj, gcomp, 1, 1)).astype(BF)

    av1[...] = mm(to_z[...], gemb).astype(BF)
    if nm > 5:
        pl.semaphore_wait(met.at[1], nq - 1)
    a1 = []
    mine = rows(zl * zrows, zrows)
    for k in range(1, nzl):
        to = (zl + k) % nzl
        a1.append(exchange(av1.at[rows(to * zrows, zrows)], av2.at[mine], dev(zl=to)))
    av2[mine] = av1[mine]

    r0.wait_recv()
    r1t = []
    for k in (1, 3, 2, 0):
        to = (y + k) % NY
        sa[to, :, tail] = (gg[:, to, c, tail].astype(F32) + rc[:, to, tail].astype(F32)).astype(BF)
        if k:
            r1t.append(reduce(sa.at[to, :, tail], ryt.at[k - 1], near_y[k]))

    for s in r1a:
        s.wait_recv()
    r2 = []
    for k in [*range(1, nx), 0]:
        at = rows(((x + k) % nx) * xa, xa)
        t = sa[y, :, at].astype(F32)
        for j in range(NY - 1):
            t += rya[j, :, at].astype(F32)
        sba[:, at] = t.astype(BF)
        if k:
            r2.append(reduce(sba.at[:, at], rxa.at[k - 1], near_x[k]))
    for s in r1b:
        s.wait_recv()
    mine = (rows(CUT + x * xd, xd), rows(DOWN + x * xu, xu), rows(DOWN + HALF + x * xu, xu))
    for k in (1, 3, 2, 0):
        to = (y + k) % NY
        t = jnp.concatenate([sa[to, :, at] for at in mine], axis=1).astype(F32)
        for j in range(nx - 1):
            t += rxb[j, to].astype(F32)
        sbb[to] = t.astype(BF)
        if k:
            r2.append(reduce(sbb.at[to], ryb.at[k - 1], near_y[k]))
    for s in r1t:
        s.wait_recv()
    t = sa[y, :, tail].astype(F32)
    for j in range(NY - 1):
        t += ryt[j].astype(F32)
    st[...] = t.astype(BF)
    r2 += [reduce(st, rxt.at[k - 1], near_x[k]) for k in range(1, nx)]
    for s in r2:
        s.wait_recv()
    ta = sba[:, rows(x * xa, xa)].astype(F32)
    for j in range(nx - 1):
        ta += rxa[j].astype(F32)
    tb = sbb[y].astype(F32)
    for j in range(NY - 1):
        tb += ryb[j].astype(F32)
    tt = st[...].astype(F32)
    for j in range(nx - 1):
        tt += rxt[j].astype(F32)
    t = jnp.concatenate([ta, tb], axis=1)
    for j in range(nq):
        sc[:, j] = jnp.concatenate([t[:, j * pq : (j + 1) * pq], tt], axis=1).astype(BF)

    r3 = []
    for k in range(1, nq):
        to = (q + k) % nq
        r3.append(reduce(sc.at[:, to], rq.at[k - 1], dev(zl=b * nq + to)))
    for s in r3:
        s.wait_recv()
    t = sc[:, q].astype(F32)
    for j in range(nq - 1):
        t += rq[j].astype(F32)
    se[...] = t.astype(BF)

    r4 = []
    for k in sorted(range(1, nm), key=lambda k: (k // nb == 0, k % nb != 0)):
        h2, b2 = (zh + k // nb) % NZH, (b + k % nb) % nb
        r4.append(reduce(se.at[h2], rb.at[k - 1], dev(zh=h2, zl=b2 * nq + q)))

    for s in a1:
        s.wait_recv()
    av3[...] = mm(to_x[...], av2[...]).astype(BF)
    a2 = []
    xrows = nzl * per
    mine = rows(x * xrows, xrows)
    for k in range(1, nx):
        to = (x + k) % nx
        a2.append(exchange(av3.at[rows(to * xrows, xrows)], av4.at[mine], near_x[k]))
    av4[mine] = av3[mine]

    for s in r4:
        s.wait_recv()
    t = se[zh].astype(F32)
    for j in range(NZH * nb - 1):
        t += rb[j].astype(F32)
    t_proj = t[pq:qp]
    ox[x, q] = t[0:pq].astype(BF)

    step = [reduce(ox.at[x, q], ox.at[x, q], dev(zl=b * nq + (q + k) % nq)) for k in range(1, nq)]
    last = [reduce(ox.at[x, q], ox.at[x, q], to) for to in near_x.values()]
    for k, copy in enumerate(step, 1):
        copy.wait_recv()
        ref = ox.at[x, (q - k + nq) % nq]
        last += [reduce(ref, ref, to) for to in near_x.values()]
    for s in a2:
        s.wait_recv()
    owned_ref[...] = av4[...]
    for s in last:
        s.wait_recv()

    scale = 1.0 / (nx * nzl * NF)

    def unit(i):
        at = i * 16
        for base, size, off in (
            (0, xa, 0), (CUT, xd, xa), (DOWN, xu, xa + xd), (DOWN + HALF, xu, xa + xd + xu)
        ):
            if base <= i * 16 < base + size * nx:
                px, at = (i * 16 - base) // size, off + (i * 16 - base) % size
        return ox[px, at // pq, at % pq : at % pq + 16, :].astype(F32) * scale

    for i in range(16):
        gdn_ref[16 * i : 16 * i + 16, 0:128] = unit(i)
        gdn_ref[16 * i : 16 * i + 16, 128:256] = unit(16 + i)
        t = unit(32 + i)
        gup_ref[:, 256 * i : 256 * i + 128] = t[0:8]
        gup_ref[:, 256 * i + 128 : 256 * i + 256] = t[8:16]
    gproj_ref[...] = t_proj * scale
    for s in pending:
        s.wait_send()


def per_device(split, embeddings, cotangent, owners, projection, up_weight, down_weight):
    nx, nzl, nq = split
    nb = nzl // nq
    feats, width = embeddings.shape[1:]
    xa = CUT // nx
    xb = (MAIN - CUT) // nx
    pq = (xa + xb) // nq
    qp = pq + ROWS - MAIN
    n_ag = 21 + 2 * (nx * NY - 1) + 3 + 2 * nx
    n_rs = 3 + 4 * (NY - 1) + 6 * (nx - 1) + 2 * (nq - 1) + (NZH * nb - 1) + nq * (nx - 1) + 3
    n_aa = nzl - 1 + nx - 1
    vmem = pl.BlockSpec(memory_space=pltpu.VMEM)
    operands = [
        pltpu.with_memory_space_constraint(a, pltpu.HBM)
        for a in (embeddings, cotangent, owners, projection, up_weight, down_weight)
    ]
    return pl.pallas_call(
        functools.partial(kernel, split),
        out_shape=(
            jax.ShapeDtypeStruct((feats, width), BF),
            jax.ShapeDtypeStruct(projection.shape, F32),
            jax.ShapeDtypeStruct(up_weight.shape, F32),
            jax.ShapeDtypeStruct(down_weight.shape, F32),
        ),
        in_specs=[pl.BlockSpec(memory_space=pl.ANY)] * 6,
        out_specs=(vmem,) * 4,
        scratch_shapes=[
            pltpu.VMEM((feats, width), BF),
            pltpu.VMEM((feats, width), BF),
            pltpu.VMEM(owners.shape, jnp.int32),
            pltpu.VMEM(up_weight.shape, BF),
            pltpu.VMEM((NZH, NY, NC, ROWS, 128), BF),
            pltpu.VMEM((NZH, NY, NC, ROWS, 128), BF),
            pltpu.VMEM((NZH, NY, ROWS, 128), BF),
            pltpu.VMEM((NY, NZH, ROWS, 128), BF),
            pltpu.VMEM((NY - 1, NZH, CUT, 128), BF),
            pltpu.VMEM((NZH, CUT, 128), BF),
            pltpu.VMEM((nx - 1, NZH, xa, 128), BF),
            pltpu.VMEM((nx - 1, NY, NZH, xb, 128), BF),
            pltpu.VMEM((NY, NZH, xb, 128), BF),
            pltpu.VMEM((NY - 1, NZH, xb, 128), BF),
            pltpu.VMEM((NY - 1, NZH, ROWS - MAIN, 128), BF),
            pltpu.VMEM((NZH, ROWS - MAIN, 128), BF),
            pltpu.VMEM((nx - 1, NZH, ROWS - MAIN, 128), BF),
            pltpu.VMEM((NZH, nq, qp, 128), BF),
            pltpu.VMEM((nq - 1, NZH, qp, 128), BF),
            pltpu.VMEM((NZH, qp, 128), BF),
            pltpu.VMEM((NZH * nb - 1, qp, 128), BF),
            pltpu.VMEM((nx, nq, pq, 128), BF),
            pltpu.VMEM((128, feats), BF),
            pltpu.VMEM((128, feats), BF),
            pltpu.VMEM((128, feats), F32),
            pltpu.VMEM((width, feats), BF),
            pltpu.VMEM((feats, feats), BF),
            pltpu.VMEM((feats, feats), BF),
            pltpu.VMEM((feats, width), BF),
            pltpu.VMEM((feats, width), BF),
            pltpu.VMEM((feats, width), BF),
            pltpu.VMEM((feats, width), BF),
            pltpu.SemaphoreType.DMA((7,)),
            pltpu.SemaphoreType.DMA((n_ag,)),
            pltpu.SemaphoreType.DMA((n_ag,)),
            pltpu.SemaphoreType.DMA((NZH * NY,)),
            pltpu.SemaphoreType.DMA((NZH * NY,)),
            pltpu.SemaphoreType.DMA((n_rs,)),
            pltpu.SemaphoreType.DMA((n_rs,)),
            pltpu.SemaphoreType.DMA((n_aa,)),
            pltpu.SemaphoreType.DMA((n_aa,)),
            pltpu.SemaphoreType.REGULAR((2,)),
        ],
        compiler_params=pltpu.CompilerParams(
            collective_id=0, has_side_effects=True, vmem_limit_bytes=48 * 1024 * 1024
        ),
        name="layer_backward",
    )(*operands)


def solution(mesh):
    return jax.shard_map(
        functools.partial(per_device, SPLITS[mesh.shape["dp"]]),
        mesh=mesh,
        in_specs=(
            P(("dp", "fsdp"), None, None),
            P(("dp", "fsdp"), None, None),
            P(("dp", "fsdp"), None),
            P("fsdp", None),
            P("fsdp", None),
            P("fsdp", None),
        ),
        out_specs=(P(("dp", "fsdp"), None), P("fsdp", None), P("fsdp", None), P("fsdp", None)),
        check_vma=False,
    )
```

```python
import functools

import jax
import jax.numpy as jnp
from jax import lax
from jax.experimental import pallas as pl
from jax.experimental.pallas import tpu as pltpu
from jax.sharding import PartitionSpec as P

BF = jnp.bfloat16
F32 = jnp.float32
SPLITS = {64: (4, 16, 4), 4: (2, 2, 2), 8: (2, 4, 2)}
NZH, NY, NC = 2, 4, 2
NF = NZH * NY * NC
MAIN, ROWS = 768, 784
CUT, DOWN = 384, 512
HALF = (MAIN - DOWN) // 2


def mm(a, b, ca=1, cb=0):
    return lax.dot_general(a, b, (((ca,), (cb,)), ((), ())), preferred_element_type=F32)


def kernel(
    split, x_hbm, cot_hbm, own_hbm, proj_hbm, up_hbm, dn_hbm,
    owned_ref, gproj_ref, gup_ref, gdn_ref,
    x_ref, cot_ref, own_ref, up_ref,
    wg, gg, rc, sa, rya, sba, rxa, rxb, sbb, ryb, ryt, st, rxt, sc, rq, se, rb, ox,
    nl, nlt, gn, half_cot, to_z, to_x, av1, av2, av3, av4,
    in_s, ag_s, ag_r, co_s, co_r, rs_s, rs_r, aa_s, aa_r, met,
):
    nx, nzl, nq = split
    nb = nzl // nq
    feats = x_ref.shape[0]
    xa, xb = rxa.shape[2], rxb.shape[3]
    xp, qp = xa + xb, se.shape[1]
    pq = xp // nq
    zrows = feats // nzl
    per = zrows // nx
    dp, fs = lax.axis_index("dp"), lax.axis_index("fsdp")
    x, zl = dp // nzl, dp % nzl
    zh, y, c = fs // (NY * NC), (fs // NC) % NY, fs % NC
    q, b = zl % nq, zl // nq

    def dev(x=x, zl=zl, zh=zh, y=y, c=c):
        return {"dp": x * nzl + zl, "fsdp": (zh * NY + y) * NC + c}

    pending = []

    def remote(src, dst, ssem, rsem, i, to):
        return pltpu.make_async_remote_copy(
            src_ref=src, dst_ref=dst, send_sem=ssem.at[i], recv_sem=rsem.at[i],
            device_id=to, device_id_type=pl.DeviceIdType.MESH,
        )

    def sender(ssem, rsem):
        count = [0]

        def send(src, dst, to):
            copy = remote(src, dst, ssem, rsem, count[0], to)
            count[0] += 1
            copy.start()
            pending.append(copy)
            return copy

        return send

    def rows(start, size):
        return pl.ds(pl.multiple_of(start, 16), size)

    gather, reduce, exchange = sender(ag_s, ag_r), sender(rs_s, rs_r), sender(aa_s, aa_r)
    sibling = dev(c=1 - c)
    near_y = {k: dev(y=(y + k) % NY) for k in (1, 3, 2)}
    near_x = {k: dev(x=(x + k) % nx) for k in range(1, nx)}

    barrier = pltpu.get_barrier_semaphore()
    peers = [sibling]
    peers += [
        dev(x=(x + i) % nx, y=(y + k) % NY) for i in range(nx) for k in range(NY) if i or k
    ]
    peers += [dev(zl=b * nq + (q + k) % nq) for k in range(1, nq)]
    m, nm = zh * nb + b, NZH * nb

    def ring(k):
        to = (m + k) % nm
        return dev(zh=to // nb, zl=(to % nb) * nq + q)

    peers += [ring(k) for k in range(1, nm) if min(k, nm - k) <= 2]
    half = (zl + nzl // 2) % nzl
    if (nzl // 2) % nq:
        peers.append(dev(zh=1 - zh, zl=half))

    def tell(i, to):
        pl.semaphore_signal(met.at[i], inc=1, device_id=to, device_id_type=pl.DeviceIdType.MESH)

    for p in peers:
        pl.semaphore_signal(barrier, inc=1, device_id=p, device_id_type=pl.DeviceIdType.MESH)

    inputs = [
        pltpu.make_async_copy(src, dst, in_s.at[i])
        for i, (src, dst) in enumerate(
            (
                (up_hbm, up_ref),
                (proj_hbm, wg.at[zh, y, c, MAIN:ROWS]),
                (dn_hbm.at[:, 0:128], wg.at[zh, y, c, 0:256]),
                (dn_hbm.at[:, 128:256], wg.at[zh, y, c, 256:512]),
                (x_hbm.at[0], x_ref),
                (own_hbm, own_ref),
                (cot_hbm.at[0], cot_ref),
            )
        )
    ]
    for copy in inputs:
        copy.start()
    inputs[0].wait()
    for u in range(NF):
        lo = up_ref[:, 256 * u : 256 * u + 128].astype(F32)
        hi = up_ref[:, 256 * u + 128 : 256 * u + 256].astype(F32)
        wg[zh, y, c, 512 + 16 * u : 528 + 16 * u] = jnp.concatenate([lo, hi], axis=0).astype(BF)
    for copy in inputs[1:4]:
        copy.wait()
    pl.semaphore_wait(barrier, len(peers))
    if nm > 5:
        tell(0, ring(2))
        tell(0, ring(nm - 2))

    parts = ((DOWN, (MAIN - DOWN) // nx), (0, DOWN // nx))
    main, tail = pl.ds(0, MAIN), pl.ds(MAIN, ROWS - MAIN)
    oz = 1 - zh
    own, other = wg.at[zh, y, c], wg.at[oz, y, c]
    far = dev(zh=oz, zl=half)

    def swap(ref, to):
        return gather(ref, ref, to)

    far_main = []
    for base, size in parts:
        far_main.append(swap(own.at[rows(base + x * size, size)], far))
        if base:
            far_tail = swap(own.at[tail], far)
    tails = [swap(own.at[tail], to) for to in near_y.values()]
    to_core = [swap(own.at[tail], sibling)]
    mains = [swap(own.at[main], to) for to in near_y.values()]
    mains_core = [swap(own.at[main], sibling)]
    for k, copy in zip(near_y, tails):
        copy.wait_recv()
        to_core.append(swap(wg.at[zh, (y - k + NY) % NY, c, tail], sibling))
    shares = {}
    for n, (base, size) in enumerate(parts):
        far_main[n].wait_recv()
        piece = rows(base + x * size, size)
        for i in range(nx):
            for k in (1, 3, 2, 0):
                if i or k:
                    shares[n, i, k] = swap(
                        other.at[piece], dev(x=(x + i) % nx, y=(y + k) % NY)
                    )
        if n == 0:
            far_tail.wait_recv()
            tails = [swap(other.at[tail], to) for to in near_y.values()]
            to_core.append(swap(other.at[tail], sibling))
    for k, copy in zip(near_y, tails):
        copy.wait_recv()
        to_core.append(swap(wg.at[oz, (y - k + NY) % NY, c, tail], sibling))
    for k, copy in zip(near_y, mains):
        copy.wait_recv()
        mains_core.append(swap(wg.at[zh, (y - k + NY) % NY, c, main], sibling))

    if nm > 5:
        pl.semaphore_wait(met.at[0], 2)
        for k in range(1, nq):
            tell(1, dev(zl=b * nq + (q + k) % nq))

    def to_sibling(n, i):
        base, size = parts[n]
        for k in range(NY):
            if i or k:
                shares[n, i, k].wait_recv()
        at = rows(base + ((x - i + nx) % nx) * size, size)
        return swap(wg.at[oz, :, c, at], sibling)

    for s in to_core:
        s.wait_recv()
    inputs[4].wait()
    emb = x_ref[...]
    proj = wg[:, :, :, MAIN:ROWS, :].reshape(feats, 128)
    compressed = mm(emb, proj, 0, 0).astype(BF)
    fm = mm(emb, compressed)
    centre = fm - jnp.mean(fm, axis=-1, keepdims=True)
    inv = lax.rsqrt(jnp.mean(centre * centre, axis=-1, keepdims=True) + 1e-05)
    normed = centre * inv
    normed_t = normed.T
    nl[...] = (0.5 * normed_t).astype(BF)
    nlt[...] = normed_t.astype(BF)
    gn[...] = jnp.zeros_like(gn)
    inputs[5].wait()
    inputs[6].wait()
    half_cot[...] = (0.5 * cot_ref[...].astype(F32)).T.astype(BF)

    row = lax.broadcasted_iota(jnp.int32, (feats, feats), 0)
    col = lax.broadcasted_iota(jnp.int32, (feats, feats), 1)
    across_f = jnp.broadcast_to(own_ref[...].astype(F32), (feats, feats))
    down_f = jnp.sum(jnp.where(row == col, across_f, 0.0), axis=1, keepdims=True)
    within = jnp.sum(
        jnp.where((across_f == down_f) & (row < col), 1.0, 0.0), axis=0, keepdims=True
    )
    owner = across_f[0:1]
    owner_x = jnp.floor(owner * (1.0 / nzl))
    place = (owner - owner_x * nzl) * zrows + owner_x * per + within
    to_z[...] = jnp.where(row.astype(F32) == place, 1.0, 0.0).astype(BF)
    r_z, r_x, r_k = col // zrows, (col % zrows) // per, col % per
    to_x[...] = jnp.where(row == r_x * (nzl * per) + r_z * per + r_k, 1.0, 0.0).astype(BF)

    mains_core += [to_sibling(0, i) for i in range(nx)]
    for s in mains_core:
        s.wait_recv()

    def hidden_units(izh, iy):
        cores = (1 - c, c)
        at = [rows(512 + 16 * ((izh * NY + iy) * NC + ic), 16) for ic in cores]
        pieces = [wg[:, :, :, r, :].reshape(NF, 16, 128).astype(F32) for r in at]
        up = jnp.concatenate(
            [p[:, e : e + 8].reshape(128, 128) for p in pieces for e in (0, 8)], axis=1
        ).astype(BF)
        downs = jnp.concatenate(
            [
                jnp.concatenate([wg[izh, iy, ic, 0:256], wg[izh, iy, ic, 256:512]], axis=1)
                for ic in cores
            ],
            axis=0,
        )
        cots = cot_ref[...]
        half_hidden = mm(up, nl[...], 0, 0)
        t1 = jnp.tanh(half_hidden) + 1.0
        act32 = half_hidden * t1
        gh = (mm(downs, half_cot[...]) * (t1 + act32 * (2.0 - t1))).astype(BF)
        gdn = mm(act32.astype(BF), cots).astype(BF)
        for e, ic in enumerate(cores):
            gg[izh, iy, ic, 0:256] = gdn[256 * e : 256 * e + 256, 0:128]
            gg[izh, iy, ic, 256:512] = gdn[256 * e : 256 * e + 256, 128:256]
        gn[...] += mm(up, gh)
        gup = mm(nlt[...], gh, 1, 1)
        for e, r in enumerate(at):
            both = [gup[:, 256 * e + h : 256 * e + h + 128].reshape(NF, 8, 128) for h in (0, 128)]
            gg[:, :, :, r, :] = (
                jnp.concatenate(both, axis=1).astype(BF).reshape(NZH, NY, NC, 16, 128)
            )

    down, first = pl.ds(0, DOWN), pl.ds(0, CUT)
    xd, xu = (DOWN - CUT) // nx, HALF // nx

    def core_copy(h, i):
        izh = (zh + h) % NZH
        return remote(
            gg.at[izh, i, 1 - c, down], rc.at[izh, i, down], co_s, co_r, h * NY + i, sibling
        )

    def hidden_loop(h):
        @pl.loop(0, NY)
        def _(i):
            izh = (zh + h) % NZH
            hidden_units(izh, i)
            core_copy(h, i).start()

    def add(at):
        sa_at, gg_at, rc_at = at
        sa[sa_at] = (gg[gg_at].astype(F32) + rc[rc_at].astype(F32)).astype(BF)

    r1a, r1b = [], []

    def upper(h):
        at = rows(DOWN + HALF * ((zh + h) % NZH), HALF)
        return reduce(gg.at[:, :, 1 - c, at], rc.at[:, :, at], sibling)

    def first_sums(h, r0):
        izh = (zh + h) % NZH
        for i in range(NY):
            core_copy(h, i).wait()
        for k in (1, 3, 2, 0):
            to = (y + k) % NY

            @pl.loop(0, CUT // 128)
            def _(i, to=to):
                r = rows(i * 128, 128)
                add(((to, izh, r), (izh, to, c, r), (izh, to, r)))

            if k:
                r1a.append(reduce(sa.at[to, izh, first], rya.at[k - 1, izh], near_y[k]))
        r0.wait_recv()
        for k in [*range(1, nx), 0]:
            to = (x + k) % nx
            lo, hi = rows(CUT + to * xd, xd), rows(DOWN + HALF * izh + to * xu, xu)

            @pl.loop(0, NY)
            def _(i, lo=lo, hi=hi):
                add(((i, izh, lo), (izh, i, c, lo), (izh, i, lo)))
                for z in range(NZH):
                    add(((i, z, hi), (z, i, c, hi), (z, i, hi)))

            if k:
                land = rxb.at[k - 1, :, izh, 0:xd]
                r1b.append(reduce(sa.at[:, izh, lo], land, near_x[k]))
                land = rxb.at[k - 1, :, :, rows(xd + xu * izh, xu)]
                r1b.append(reduce(sa.at[:, :, hi], land, near_x[k]))

    hidden_loop(0)
    r0 = upper(0)
    first_sums(0, r0)
    late = [to_sibling(1, i) for i in range(nx)]
    for s in late:
        s.wait_recv()
    hidden_loop(1)
    r0 = upper(1)
    first_sums(1, r0)

    gnorm = gn[...].T
    gfm = inv * (
        gnorm
        - jnp.mean(gnorm, axis=-1, keepdims=True)
        - normed * jnp.mean(gnorm * normed, axis=-1, keepdims=True)
    )
    gfm = gfm.astype(BF)
    gcomp = mm(emb, gfm, 0, 0).astype(BF)
    gproj = mm(emb, gcomp).astype(BF)
    gg[:, :, :, MAIN:ROWS, :] = gproj.reshape(NZH, NY, NC, 16, 128)
    r0 = reduce(gg.at[:, :, 1 - c, tail], rc.at[:, :, tail], sibling)
    r0.wait_recv()
    r1t = []
    for k in (1, 3, 2, 0):
        to = (y + k) % NY
        sa[to, :, tail] = (gg[:, to, c, tail].astype(F32) + rc[:, to, tail].astype(F32)).astype(BF)
        if k:
            r1t.append(reduce(sa.at[to, :, tail], ryt.at[k - 1], near_y[k]))

    for s in r1a:
        s.wait_recv()
    r2 = []
    for k in [*range(1, nx), 0]:
        at = rows(((x + k) % nx) * xa, xa)
        t = sa[y, :, at].astype(F32)
        for j in range(NY - 1):
            t += rya[j, :, at].astype(F32)
        sba[:, at] = t.astype(BF)
        if k:
            r2.append(reduce(sba.at[:, at], rxa.at[k - 1], near_x[k]))
    for s in r1b:
        s.wait_recv()
    mine = (rows(CUT + x * xd, xd), rows(DOWN + x * xu, xu), rows(DOWN + HALF + x * xu, xu))
    for k in (1, 3, 2, 0):
        to = (y + k) % NY
        t = jnp.concatenate([sa[to, :, at] for at in mine], axis=1).astype(F32)
        for j in range(nx - 1):
            t += rxb[j, to].astype(F32)
        sbb[to] = t.astype(BF)
        if k:
            r2.append(reduce(sbb.at[to], ryb.at[k - 1], near_y[k]))
    for s in r1t:
        s.wait_recv()
    t = sa[y, :, tail].astype(F32)
    for j in range(NY - 1):
        t += ryt[j].astype(F32)
    st[...] = t.astype(BF)
    r2 += [reduce(st, rxt.at[k - 1], near_x[k]) for k in range(1, nx)]
    gemb = (mm(gfm, compressed, 1, 1) + mm(proj, gcomp, 1, 1)).astype(BF)

    av1[...] = mm(to_z[...], gemb).astype(BF)
    if nm > 5:
        pl.semaphore_wait(met.at[1], nq - 1)
    a1 = []
    mine = rows(zl * zrows, zrows)
    for k in range(1, nzl):
        to = (zl + k) % nzl
        a1.append(exchange(av1.at[rows(to * zrows, zrows)], av2.at[mine], dev(zl=to)))
    av2[mine] = av1[mine]

    for s in r2:
        s.wait_recv()
    ta = sba[:, rows(x * xa, xa)].astype(F32)
    for j in range(nx - 1):
        ta += rxa[j].astype(F32)
    tb = sbb[y].astype(F32)
    for j in range(NY - 1):
        tb += ryb[j].astype(F32)
    tt = st[...].astype(F32)
    for j in range(nx - 1):
        tt += rxt[j].astype(F32)
    t = jnp.concatenate([ta, tb], axis=1)
    for j in range(nq):
        sc[:, j] = jnp.concatenate([t[:, j * pq : (j + 1) * pq], tt], axis=1).astype(BF)

    r3 = []
    for k in range(1, nq):
        to = (q + k) % nq
        r3.append(reduce(sc.at[:, to], rq.at[k - 1], dev(zl=b * nq + to)))
    for s in r3:
        s.wait_recv()
    t = sc[:, q].astype(F32)
    for j in range(nq - 1):
        t += rq[j].astype(F32)
    se[...] = t.astype(BF)

    r4 = []
    for k in sorted(range(1, nm), key=lambda k: (k // nb == 0, k % nb != 0)):
        h2, b2 = (zh + k // nb) % NZH, (b + k % nb) % nb
        r4.append(reduce(se.at[h2], rb.at[k - 1], dev(zh=h2, zl=b2 * nq + q)))

    for s in a1:
        s.wait_recv()
    av3[...] = mm(to_x[...], av2[...]).astype(BF)
    a2 = []
    xrows = nzl * per
    mine = rows(x * xrows, xrows)
    for k in range(1, nx):
        to = (x + k) % nx
        a2.append(exchange(av3.at[rows(to * xrows, xrows)], av4.at[mine], near_x[k]))
    av4[mine] = av3[mine]

    for s in r4:
        s.wait_recv()
    t = se[zh].astype(F32)
    for j in range(NZH * nb - 1):
        t += rb[j].astype(F32)
    t_proj = t[pq:qp]
    ox[x, q] = t[0:pq].astype(BF)

    step = [reduce(ox.at[x, q], ox.at[x, q], dev(zl=b * nq + (q + k) % nq)) for k in range(1, nq)]
    last = [reduce(ox.at[x, q], ox.at[x, q], to) for to in near_x.values()]
    for k, copy in enumerate(step, 1):
        copy.wait_recv()
        ref = ox.at[x, (q - k + nq) % nq]
        last += [reduce(ref, ref, to) for to in near_x.values()]
    for s in a2:
        s.wait_recv()
    owned_ref[...] = av4[...]
    for s in last:
        s.wait_recv()

    scale = 1.0 / (nx * nzl * NF)

    def unit(i):
        at = i * 16
        for base, size, off in (
            (0, xa, 0), (CUT, xd, xa), (DOWN, xu, xa + xd), (DOWN + HALF, xu, xa + xd + xu)
        ):
            if base <= i * 16 < base + size * nx:
                px, at = (i * 16 - base) // size, off + (i * 16 - base) % size
        return ox[px, at // pq, at % pq : at % pq + 16, :].astype(F32) * scale

    for i in range(16):
        gdn_ref[16 * i : 16 * i + 16, 0:128] = unit(i)
        gdn_ref[16 * i : 16 * i + 16, 128:256] = unit(16 + i)
        t = unit(32 + i)
        gup_ref[:, 256 * i : 256 * i + 128] = t[0:8]
        gup_ref[:, 256 * i + 128 : 256 * i + 256] = t[8:16]
    gproj_ref[...] = t_proj * scale
    for s in pending:
        s.wait_send()


def per_device(split, embeddings, cotangent, owners, projection, up_weight, down_weight):
    nx, nzl, nq = split
    nb = nzl // nq
    feats, width = embeddings.shape[1:]
    xa = CUT // nx
    xb = (MAIN - CUT) // nx
    pq = (xa + xb) // nq
    qp = pq + ROWS - MAIN
    n_ag = 21 + 2 * (nx * NY - 1) + 3 + 2 * nx
    n_rs = 3 + 4 * (NY - 1) + 6 * (nx - 1) + 2 * (nq - 1) + (NZH * nb - 1) + nq * (nx - 1) + 3
    n_aa = nzl - 1 + nx - 1
    vmem = pl.BlockSpec(memory_space=pltpu.VMEM)
    operands = [
        pltpu.with_memory_space_constraint(a, pltpu.HBM)
        for a in (embeddings, cotangent, owners, projection, up_weight, down_weight)
    ]
    return pl.pallas_call(
        functools.partial(kernel, split),
        out_shape=(
            jax.ShapeDtypeStruct((feats, width), BF),
            jax.ShapeDtypeStruct(projection.shape, F32),
            jax.ShapeDtypeStruct(up_weight.shape, F32),
            jax.ShapeDtypeStruct(down_weight.shape, F32),
        ),
        in_specs=[pl.BlockSpec(memory_space=pl.ANY)] * 6,
        out_specs=(vmem,) * 4,
        scratch_shapes=[
            pltpu.VMEM((feats, width), BF),
            pltpu.VMEM((feats, width), BF),
            pltpu.VMEM(owners.shape, jnp.int32),
            pltpu.VMEM(up_weight.shape, BF),
            pltpu.VMEM((NZH, NY, NC, ROWS, 128), BF),
            pltpu.VMEM((NZH, NY, NC, ROWS, 128), BF),
            pltpu.VMEM((NZH, NY, ROWS, 128), BF),
            pltpu.VMEM((NY, NZH, ROWS, 128), BF),
            pltpu.VMEM((NY - 1, NZH, CUT, 128), BF),
            pltpu.VMEM((NZH, CUT, 128), BF),
            pltpu.VMEM((nx - 1, NZH, xa, 128), BF),
            pltpu.VMEM((nx - 1, NY, NZH, xb, 128), BF),
            pltpu.VMEM((NY, NZH, xb, 128), BF),
            pltpu.VMEM((NY - 1, NZH, xb, 128), BF),
            pltpu.VMEM((NY - 1, NZH, ROWS - MAIN, 128), BF),
            pltpu.VMEM((NZH, ROWS - MAIN, 128), BF),
            pltpu.VMEM((nx - 1, NZH, ROWS - MAIN, 128), BF),
            pltpu.VMEM((NZH, nq, qp, 128), BF),
            pltpu.VMEM((nq - 1, NZH, qp, 128), BF),
            pltpu.VMEM((NZH, qp, 128), BF),
            pltpu.VMEM((NZH * nb - 1, qp, 128), BF),
            pltpu.VMEM((nx, nq, pq, 128), BF),
            pltpu.VMEM((128, feats), BF),
            pltpu.VMEM((128, feats), BF),
            pltpu.VMEM((128, feats), F32),
            pltpu.VMEM((width, feats), BF),
            pltpu.VMEM((feats, feats), BF),
            pltpu.VMEM((feats, feats), BF),
            pltpu.VMEM((feats, width), BF),
            pltpu.VMEM((feats, width), BF),
            pltpu.VMEM((feats, width), BF),
            pltpu.VMEM((feats, width), BF),
            pltpu.SemaphoreType.DMA((7,)),
            pltpu.SemaphoreType.DMA((n_ag,)),
            pltpu.SemaphoreType.DMA((n_ag,)),
            pltpu.SemaphoreType.DMA((NZH * NY,)),
            pltpu.SemaphoreType.DMA((NZH * NY,)),
            pltpu.SemaphoreType.DMA((n_rs,)),
            pltpu.SemaphoreType.DMA((n_rs,)),
            pltpu.SemaphoreType.DMA((n_aa,)),
            pltpu.SemaphoreType.DMA((n_aa,)),
            pltpu.SemaphoreType.REGULAR((2,)),
        ],
        compiler_params=pltpu.CompilerParams(
            collective_id=0, has_side_effects=True, vmem_limit_bytes=48 * 1024 * 1024
        ),
        name="layer_backward",
    )(*operands)


def solution(mesh):
    return jax.shard_map(
        functools.partial(per_device, SPLITS[mesh.shape["dp"]]),
        mesh=mesh,
        in_specs=(
            P(("dp", "fsdp"), None, None),
            P(("dp", "fsdp"), None, None),
            P(("dp", "fsdp"), None),
            P("fsdp", None),
            P("fsdp", None),
            P("fsdp", None),
        ),
        out_specs=(P(("dp", "fsdp"), None), P("fsdp", None), P("fsdp", None), P("fsdp", None)),
        check_vma=False,
    )
```
